768 devices in a mesh: gx: 96 (over z, x, core), gy: 8 (over y).
Axes of the slice: x: 4, y: 8, z: 12, core: 2. Of those that a mesh axis runs over, the one named last changes fastest.
Arguments:
- blocks: float32 [6144, 64, 448], P(('gx', 'gy')), may hold values from -0.75 to 0.75
- neighbors: int32 [6144, 7], P(('gx', 'gy')), may hold values from 0 to 6143, as said below
- aggregate: int32 [6144], P(('gx', 'gy')), may hold values from 0 to 1535, as said below
- tentative: float32 [64, 393216], P(None, ('gx', 'gy')), may hold values from -0.75 to 0.75
- inv_diagonal: float32 [64, 393216], P(None, ('gx', 'gy')), may hold values from -0.75 to 0.75
- target: int32 [1536], P(('gx', 'gy')), may hold values from 0 to 7, as said below
Outputs:
- repart: float32 [393216, 640], P(('gx', 'gy'))
- anchor: int32 [6144], P(('gx', 'gy'))
The draws below stay inside these ranges and needn't reach their ends.
Inputs may be any that keep to these rules, and one draw needn't show every extreme that they name: `neighbors`: row i lists i first, then 7 - 1 block columns j with 1 <= |j - i| <= 4 (repeats may occur next to the ends of the grid); the distance 4 occurs. Each block row belongs to an aggregate of its own device: i // 8 == aggregate[i] // 2; every aggregate holds one block row or more. `target`: the 2 coarse rows of one device name distinct positions; in each group of 8 consecutive devices one position is named by every device of the group.
All inputs are finite; a program needn't handle non-finite values.
Results may differ from the reference program's by a relative error of at most 0.0003.
Values sent between devices are 32-bit elements; how exact they have to be, the bound alone decides.
No kernel may reach another device: no remote copies, remote signals or barrier semaphores. Data moves between devices by JAX's collectives and lax.ppermute only.
A program may use at most 64 MiB of HBM per device.

```python
import jax
import jax.numpy as jnp
from jax import lax

BS = 64
K = 7
RB = 8
NA = 2
REACH = 4
AW = 640
NB = 6144
NAG = 1536
N_GX = 96
N_GY = 8
DEVICES = 768


def draw_neighbors(key, part):
    key = jax.random.fold_in(key, 11)
    row_ids = jnp.arange(NB, dtype=jnp.int32)
    steps_up = jnp.arange(1, REACH + 1, dtype=jnp.int32)
    offset_pool = jnp.concatenate([steps_up, -steps_up])
    row_keys = jax.random.split(key, NB)
    shuffled = jax.vmap(lambda row_key: jax.random.permutation(row_key, offset_pool))(row_keys)
    offsets = shuffled[:, :K - 1]
    position = row_ids % RB
    offsets = offsets.at[:, 0].set(jnp.where(position == RB - 1, REACH, offsets[:, 0]))
    offsets = offsets.at[:, 1].set(jnp.where(position == 0, -REACH, offsets[:, 1]))
    columns = row_ids[:, None] + offsets
    outside = (columns < 0) | (columns >= NB)
    columns = jnp.where(outside, row_ids[:, None] - offsets, columns)
    return jnp.concatenate([row_ids[:, None], columns], 1).astype(jnp.int32)


def draw_aggregate(key, part):
    key = jax.random.fold_in(key, 12)
    raw_key, pick_key = jax.random.split(key)
    raw_draw = jax.random.randint(raw_key, (DEVICES, RB), 0, NA * NA)
    levels = jnp.arange(1, NA, dtype=jnp.int32)
    member = jnp.sum((raw_draw[:, :, None] >= (levels * levels)[None, None, :]).astype(jnp.int32), axis=2)
    device_keys = jax.random.split(pick_key, DEVICES)
    picked = jax.vmap(lambda device_key: jax.random.permutation(device_key, RB))(device_keys)[:, :NA]
    hit_mask = picked[:, :, None] == jnp.arange(RB, dtype=jnp.int32)[None, None, :]
    forced = jnp.sum(hit_mask.astype(jnp.int32) * jnp.arange(NA, dtype=jnp.int32)[None, :, None], axis=1)
    member = jnp.where(jnp.any(hit_mask, axis=1), forced, member)
    owners = jnp.arange(DEVICES, dtype=jnp.int32)[:, None] * NA
    return (owners + member).reshape(NB).astype(jnp.int32)


def draw_target(key, part):
    key = jax.random.fold_in(key, 13)
    first_key, other_key = jax.random.split(key)
    group_total = DEVICES // N_GY
    first_pos = jax.random.randint(first_key, (group_total,), 0, N_GY)
    device_keys = jax.random.split(other_key, DEVICES)
    other_pos = jax.vmap(lambda device_key: jax.random.permutation(device_key, N_GY - 1))(device_keys)
    first_dev = jnp.repeat(first_pos, N_GY)
    rest_pos = (first_dev[:, None] + 1 + other_pos) % N_GY
    targets = jnp.concatenate([first_dev[:, None], rest_pos[:, :NA - 1]], 1)
    return targets.reshape(NAG).astype(jnp.int32)


def level_of(key, dims, cuts, smallest, top_value):
    level, own = 1.0, jax.random.fold_in(key, 6)
    for axis_at, blocks in cuts:
        draws = jnp.exp(jax.random.uniform(jax.random.fold_in(own, axis_at), (blocks,), jnp.float32, smallest / len(cuts), top_value / len(cuts)))
        level = level * jnp.repeat(draws, dims[axis_at] // blocks).reshape([-1 if axis == axis_at else 1 for axis in range(len(dims))])
    return level


def noise(key, dims, deviation, most, cuts=(), kind=jnp.bfloat16):
    entries = jax.random.normal(key, dims, jnp.float32) * deviation
    if len(cuts) > 0:
        entries = level_of(key, dims, cuts, -0.22, 0.18) * entries
    return jnp.clip(entries, min=-most, max=most).astype(kind)


def setup_inputs(seed: int = 0) -> dict:
    streams_of = jax.random.split(jax.random.key(seed), 7)
    blocks = noise(streams_of[0], (NB, BS, K * BS), BS ** -0.5, 0.75, ((0, 768),), jnp.float32)
    neighbors = draw_neighbors(jax.random.fold_in(streams_of[6], 71), 0)
    aggregate = draw_aggregate(jax.random.fold_in(streams_of[6], 71), 0)
    tentative = noise(streams_of[3], (BS, NB * BS), BS ** -0.5, 0.75, ((1, 768),), jnp.float32)
    inv_diagonal = noise(streams_of[4], (BS, NB * BS), BS ** -0.5, 0.75, ((1, 768),), jnp.float32)
    target = draw_target(jax.random.fold_in(streams_of[6], 71), 0)
    return dict(blocks=blocks, neighbors=neighbors, aggregate=aggregate, tentative=tentative, inv_diagonal=inv_diagonal, target=target)


OMEGA = 2.0 / 3.0
HIGHEST = lax.Precision.HIGHEST


def smooth_rows(matrix, dinv_rows, tent_own, agg_own, near_index, tent_near, agg_near, agg_base, windows):
    row_total = matrix.shape[0]
    block_size = matrix.shape[1]
    near_tent = tent_near[near_index]
    product = jnp.einsum('irkc,ikcs->ikrs', matrix, near_tent, precision=HIGHEST)
    columns = jnp.arange(windows, dtype=jnp.int32)
    placed = ((agg_near[near_index] - agg_base)[:, :, None] == columns[None, None, :]).astype(jnp.float32)
    summed = jnp.einsum('ikw,ikrs->irws', placed, product, precision=HIGHEST).reshape(row_total, block_size, windows * block_size)
    smoothed = jnp.einsum('irc,icp->irp', dinv_rows, summed, precision=HIGHEST)
    initial_hot = ((agg_own - agg_base)[:, None] == columns[None, :]).astype(jnp.float32)
    initial = jnp.einsum('iw,irs->irws', initial_hot, tent_own, precision=HIGHEST).reshape(row_total, block_size, windows * block_size)
    return initial - OMEGA * smoothed


def neighbours_rows(per_device, device, width):
    lower_rows = per_device[jnp.maximum(device - 1, 0)][RB - width:]
    upper_rows = per_device[jnp.minimum(device + 1, DEVICES - 1)][:width]
    lower_rows = jnp.where(device > 0, lower_rows, jnp.zeros_like(lower_rows))
    upper_rows = jnp.where(device < DEVICES - 1, upper_rows, jnp.zeros_like(upper_rows))
    return jnp.concatenate([lower_rows, per_device[device], upper_rows], 0)


def reference(blocks, neighbors, aggregate, tentative, inv_diagonal, target):
    agg_cols = NA * BS
    matrix_all = blocks.reshape(DEVICES, RB, BS, K, BS)
    nbr_all = neighbors.reshape(DEVICES, RB, K)
    agg_all = aggregate.reshape(DEVICES, RB)
    tent_all = tentative.reshape(BS, DEVICES, RB, BS).transpose(1, 2, 0, 3)
    dinv_all = inv_diagonal.reshape(BS, DEVICES, RB, BS).transpose(1, 2, 0, 3)
    device_ids = jnp.arange(DEVICES, dtype=jnp.int32)

    def prolong_one(device):
        first_row = device * RB
        tent_near = neighbours_rows(tent_all, device, REACH)
        agg_near = neighbours_rows(agg_all, device, REACH)
        near_index = (nbr_all[device] - first_row + REACH).astype(jnp.int32)
        return smooth_rows(matrix_all[device], dinv_all[device], tent_all[device], agg_all[device],
                           near_index, tent_near, agg_near, (device - 1) * NA, 3 * NA)

    prolong_all = lax.map(prolong_one, device_ids)

    def partial_one(device):
        first_row = device * RB
        near_rows = neighbours_rows(prolong_all, device, REACH)
        framed = jnp.concatenate([
            jnp.pad(near_rows[:REACH], ((0, 0), (0, 0), (0, 2 * agg_cols))),
            jnp.pad(near_rows[REACH:REACH + RB], ((0, 0), (0, 0), (agg_cols, agg_cols))),
            jnp.pad(near_rows[REACH + RB:], ((0, 0), (0, 0), (2 * agg_cols, 0)))], 0)
        near_index = (nbr_all[device] - first_row + REACH).astype(jnp.int32)
        matrix = matrix_all[device]
        applied = jnp.zeros((RB, BS, AW), jnp.float32)
        for column_slot in range(K):
            applied = applied + jnp.einsum('irc,icq->irq', matrix[:, :, column_slot, :],
                                           framed[near_index[:, column_slot]], precision=HIGHEST)
        return jnp.einsum('irp,irq->pq', prolong_all[device], applied, precision=HIGHEST)

    partial_all = lax.map(partial_one, device_ids)
    middle = partial_all[:, agg_cols:2 * agg_cols]
    from_lower = jnp.pad(partial_all[:-1, 2 * agg_cols:, agg_cols:], ((1, 0), (0, 0), (0, agg_cols)))
    from_upper = jnp.pad(partial_all[1:, :agg_cols, :4 * agg_cols], ((0, 1), (0, 0), (agg_cols, 0)))
    coarse_band = middle + from_lower + from_upper

    band_rows = coarse_band.reshape(N_GX, N_GY, NA, BS, AW)
    chosen = target.reshape(N_GX, N_GY, NA)[:, :, :, None] == jnp.arange(N_GY, dtype=jnp.int32)[None, None, None, :]
    repart = jnp.einsum('xsuy,xsubq->xysbq', chosen.astype(jnp.float32), band_rows,
                        precision=HIGHEST).reshape(DEVICES * N_GY * BS, AW)
    coarse_ids = jnp.arange(NAG, dtype=jnp.int32).reshape(N_GX, N_GY, NA) + 1
    anchor = jnp.sum(chosen.astype(jnp.int32) * coarse_ids[:, :, :, None], axis=2) - 1
    anchor = anchor.transpose(0, 2, 1).reshape(DEVICES * N_GY).astype(jnp.int32)
    return repart, anchor
```

```python
import jax
import jax.numpy as jnp
from jax import lax
from jax.experimental import pallas as pl
from jax.experimental.pallas import tpu as pltpu
from jax.sharding import PartitionSpec as P

BS = 64
K = 7
RB = 8
NA = 2
AW = 640
HALF = 256
AGG = NA * BS
EDGE = 9 * BS + 8
SLOT = 5 * BS + 8
OMEGA = 2.0 / 3.0
F32 = jnp.float32
BF16 = jnp.bfloat16


def split(x):
    high = x.astype(BF16)
    return high, (x - high.astype(F32)).astype(BF16)


def dot3(a, b, side=1):
    def dot(x, y):
        return lax.dot_general(x, y, (((side,), (0,)), ((), ())), preferred_element_type=F32)

    return dot(a[0], b[0]) + (dot(a[0], b[1]) + dot(a[1], b[0]))


def lane_half(rows):
    return lax.broadcasted_iota(jnp.int32, (rows, 2 * BS), 1) // BS


def doubled(pair):
    low = lane_half(BS) == 0
    other = pltpu.roll(pair, BS, 1)
    return jnp.where(low, pair, other), jnp.where(low, other, pair)


def place(pairs, members):
    half = lane_half(BS)
    rows = []
    for p, pair in enumerate(pairs):
        for q, block in enumerate(doubled(pair)):
            rows.append(jnp.where(half == members[2 * p + q], block, 0.0))
    return jnp.concatenate(rows, 0)


def block_diagonal(low, high):
    tall = jnp.concatenate([jnp.concatenate([low, high], 1)] * 4, 0)
    row = lax.broadcasted_iota(jnp.int32, tall.shape, 0) // BS
    column = lax.broadcasted_iota(jnp.int32, tall.shape, 1) // BS
    return jnp.where(row == column, tall, 0.0)


def piece(ref, c):
    return ref[c * BS : (c + 1) * BS]


def received_members(ref):
    return [ref[9 * BS + m : 9 * BS + m + 1].astype(jnp.int32) for m in range(4)]


def received_place(ref):
    return place([piece(ref, 0), piece(ref, 1)], received_members(ref))


def frame_columns(frame, first, columns):
    return jnp.concatenate([frame[first : first + 4, c].reshape(HALF, 2 * BS) for c in columns], 1)


def frame_kernel(nbr, agg, blocks, tent, dinv, frame, up, down):
    first = nbr[0, 0]
    half = lane_half(BS)
    for i in range(RB):
        origin = first - 4 if i < 4 else first
        mine = i + 4 if i < 4 else i
        copies = []
        for p in range(3):
            copies.extend(doubled(blocks[i, :, 2 * p * BS : 2 * (p + 1) * BS]))
        last = blocks[i, :, 6 * BS : 7 * BS]
        copies.append(jnp.concatenate([last, last], 1))
        for c in range(6):
            if c == mine // 2:
                frame[i, c] = jnp.where(half == mine % 2, copies[0], 0.0)
            else:
                frame[i, c] = jnp.zeros((BS, 2 * BS), F32)
        for k in range(1, K):
            at = nbr[i, k] - origin
            column = at >> 1
            frame[i, column] = frame[i, column] + jnp.where(half == (at & 1), copies[k], 0.0)

    def send(out, pieces, members):
        for c, value in enumerate(pieces):
            out[c * BS : (c + 1) * BS] = value
        row = lax.broadcasted_iota(jnp.int32, (8, 2 * BS), 0)
        value = jnp.zeros((8, 2 * BS), F32)
        for m, member in enumerate(members):
            value = jnp.where(row == m, member.astype(F32), value)
        out[9 * BS :] = value

    owner = first // 4
    low = half == 0
    send(
        up,
        [tent[:, 256:384], tent[:, 384:512], dinv[:, 256:384], dinv[:, 384:512]]
        + [frame[7, 4], frame[7, 5], frame[6, 4]]
        + [jnp.where(low, frame[6, 5], pltpu.roll(frame[4, 4], BS, 1)), frame[5, 4]],
        [agg[4 + m] - owner for m in range(4)],
    )
    send(
        down,
        [tent[:, 0:128], tent[:, 128:256], dinv[:, 0:128], dinv[:, 128:256]]
        + [frame[0, 0], frame[0, 1]]
        + [jnp.where(low, pltpu.roll(frame[3, 1], BS, 1), frame[1, 0]), frame[1, 1], frame[2, 1]],
        [agg[m] - owner for m in range(4)],
    )


def own_kernel(nbr, agg, frame, tent, dinv, a_high, a_low, near, factors, own, image):
    owner = nbr[0, 0] // 4
    a = split(
        jnp.concatenate(
            [frame_columns(frame, 0, range(2, 6)), frame_columns(frame, 4, range(0, 4))], 0
        )
    )
    a_high[...], a_low[...] = a
    placed = place(
        [tent[:, 2 * p * BS : 2 * (p + 1) * BS] for p in range(4)],
        [agg[j] - owner for j in range(RB)],
    )
    near[...] = placed
    summed = dot3(a, split(placed))
    parts = []
    for s, columns in ((0, (0, 1)), (1, (4, 5))):
        rows = slice(s * HALF, (s + 1) * HALF)
        inverse = split(
            block_diagonal(
                dinv[:, s * HALF : s * HALF + 128], dinv[:, s * HALF + 128 : (s + 1) * HALF]
            )
        )
        parts.append(placed[rows] - OMEGA * dot3(inverse, split(summed[rows])))
        factors[s] = -OMEGA * dot3(inverse, split(frame_columns(frame, 4 * s, columns)))
    prolong = jnp.concatenate(parts, 0)
    own[...] = prolong
    image[...] = dot3(a, split(prolong))


def edge_kernel(a_high, a_low, factors, own, image, below, above, side, left, right, up, down):
    b_low = dot3(split(factors[0]), split(received_place(below)))
    b_high = dot3(split(factors[1]), split(received_place(above)))
    side[:HALF] = b_low
    side[HALF:] = b_high
    b_low, b_high = split(b_low), split(b_high)
    image_left = dot3((a_high[:, :HALF], a_low[:, :HALF]), b_low)
    image_right = dot3((a_high[:, HALF:], a_low[:, HALF:]), b_high)
    left[...] = image_left
    right[...] = image_right
    for out, factor, rows in ((down, b_low, slice(0, HALF)), (up, b_high, slice(HALF, 2 * HALF))):
        terms = dot3(
            factor,
            split(jnp.concatenate([image_left[rows], image[rows], image_right[rows]], 1)),
            0,
        )
        for c in range(3):
            out[c * AGG : (c + 1) * AGG] = terms[:, c * AGG : (c + 1) * AGG]
        out[3 * AGG :] = own[rows]


def middle_kernel(frame, near, own, image, side, left, right, below, above, part, lo, hi):
    own_low, own_high = own[:HALF], own[HALF:]
    c_low, c_high = split(own_low), split(own_high)
    middle = dot3(
        split(own[...]), split(jnp.concatenate([left[...], image[...], right[...]], 1)), 0
    )
    low = lane_half(BS) == 0
    none = jnp.zeros((BS, 2 * BS), F32)

    def square(rows):
        return split(jnp.concatenate([jnp.concatenate(row, 1) for row in rows], 0))

    seven = piece(below, 7)
    a_below = square(
        [
            [jnp.where(low, pltpu.roll(seven, BS, 1), 0.0), none],
            [piece(below, 8), none],
            [piece(below, 6), jnp.where(low, seven, 0.0)],
            [piece(below, 4), piece(below, 5)],
        ]
    )
    six = piece(above, 6)
    a_above = square(
        [
            [piece(above, 4), piece(above, 5)],
            [jnp.where(low, 0.0, six), piece(above, 7)],
            [none, piece(above, 8)],
            [none, jnp.where(low, 0.0, pltpu.roll(six, BS, 1))],
        ]
    )
    inverse = split(block_diagonal(piece(below, 2), piece(below, 3)))
    b_below = split(
        -OMEGA * dot3(inverse, split(dot3(a_below, split(near[:HALF]))))
    )
    inverse = split(block_diagonal(piece(above, 2), piece(above, 3)))
    b_above = split(
        -OMEGA * dot3(inverse, split(dot3(a_above, split(near[HALF:]))))
    )
    x_low = dot3(
        b_below, split(dot3(a_below, split(jnp.concatenate([side[:HALF], own_low], 1)))), 0
    )
    x_high = dot3(
        b_above, split(dot3(a_above, split(jnp.concatenate([own_high, side[HALF:]], 1)))), 0
    )
    t_low = dot3(c_low, split(frame_columns(frame, 0, (0, 1))), 0)
    t_high = dot3(c_high, split(frame_columns(frame, 4, (4, 5))), 0)
    lo[...] = t_low
    hi[...] = t_high
    part[:, :AGG] = middle[:, :AGG] + x_low[:, :AGG]
    part[:, AGG : 2 * AGG] = (
        middle[:, AGG : 2 * AGG]
        + (x_low[:, AGG:] + dot3(split(t_low), b_below))
        + (x_high[:, :AGG] + dot3(split(t_high), b_above))
    )
    part[:, 2 * AGG :] = middle[:, 2 * AGG :] + x_high[:, AGG:]


def finish_kernel(nbr, target, part, lo, hi, below, above, out):
    first_id = nbr[0, 0] // 4
    band = [
        below[:AGG],
        part[:, :AGG]
        + below[AGG : 2 * AGG]
        + dot3(split(lo[...]), split(below[3 * AGG :])),
        part[:, AGG : 2 * AGG] + below[2 * AGG : 3 * AGG] + above[:AGG],
        part[:, 2 * AGG :]
        + above[AGG : 2 * AGG]
        + dot3(split(hi[...]), split(above[3 * AGG :])),
        above[2 * AGG : 3 * AGG],
    ]
    for g in range(RB):
        out[g] = jnp.zeros((SLOT, 2 * BS), F32)
    for u in range(NA):
        g = target[u]
        for c in range(5):
            out[g, c * BS : (c + 1) * BS] = band[c][u * BS : (u + 1) * BS]
        out[g, 5 * BS :] = jnp.full((8, 2 * BS), first_id + (u + 1), jnp.int32).astype(F32)


def unpack_kernel(got, rows, ids):
    lane = lax.broadcasted_iota(jnp.int32, (1, 2 * BS), 1)
    found = jnp.zeros((1, 2 * BS), F32)
    for s in range(RB):
        for c in range(5):
            rows[s * BS : (s + 1) * BS, c * 128 : (c + 1) * 128] = got[s, c * BS : (c + 1) * BS]
        found = jnp.where(lane == s, got[s, 5 * BS : 5 * BS + 1], found)
    ids[...] = found.astype(jnp.int32) - 1


VMEM = pl.BlockSpec(memory_space=pltpu.VMEM)
SMEM = pl.BlockSpec(memory_space=pltpu.SMEM)


def call(kernel, scalars, arrays, outs):
    return pl.pallas_call(
        kernel,
        in_specs=[SMEM] * len(scalars) + [VMEM] * len(arrays),
        out_specs=[VMEM] * len(outs),
        out_shape=[jax.ShapeDtypeStruct(shape, dtype) for shape, dtype in outs],
        compiler_params=pltpu.CompilerParams(vmem_limit_bytes=32 * 1024 * 1024),
        name=kernel.__name__,
    )(*scalars, *arrays)


def body(blocks, neighbors, aggregate, tentative, inv_diagonal, target):
    axes = ("gx", "gy")
    devices = lax.axis_size(axes)
    upward = [(i, i + 1) for i in range(devices - 1)]
    downward = [(j, i) for i, j in upward]
    frame, up, down = call(
        frame_kernel,
        [neighbors, aggregate],
        [blocks, tentative, inv_diagonal],
        [((RB, 6, BS, 2 * BS), F32), ((EDGE, 2 * BS), F32), ((EDGE, 2 * BS), F32)],
    )
    below = lax.ppermute(up, axes, upward)
    above = lax.ppermute(down, axes, downward)
    a_high, a_low, near, factors, own, image = call(
        own_kernel,
        [neighbors, aggregate],
        [frame, tentative, inv_diagonal],
        [
            ((2 * HALF, 2 * HALF), BF16),
            ((2 * HALF, 2 * HALF), BF16),
            ((2 * HALF, AGG), F32),
            ((2, HALF, HALF), F32),
            ((2 * HALF, AGG), F32),
            ((2 * HALF, AGG), F32),
        ],
    )
    side, left, right, up, down = call(
        edge_kernel,
        [],
        [a_high, a_low, factors, own, image, below, above],
        [((2 * HALF, AGG), F32)] * 3 + [((5 * AGG, AGG), F32)] * 2,
    )
    below_terms = lax.ppermute(up, axes, upward)
    above_terms = lax.ppermute(down, axes, downward)
    part, lo, hi = call(
        middle_kernel,
        [],
        [frame, near, own, image, side, left, right, below, above],
        [((AGG, 3 * AGG), F32), ((AGG, HALF), F32), ((AGG, HALF), F32)],
    )
    (slots,) = call(
        finish_kernel,
        [neighbors, target],
        [part, lo, hi, below_terms, above_terms],
        [((RB, SLOT, 2 * BS), F32)],
    )
    got = lax.all_to_all(slots, "gy", split_axis=0, concat_axis=0, tiled=True)
    rows, ids = call(
        unpack_kernel,
        [],
        [got],
        [((RB * BS, AW), F32), ((1, 2 * BS), jnp.int32)],
    )
    return rows, ids[0, :RB]


def solution(mesh):
    placed = (
        P(("gx", "gy"), None, None),
        P(("gx", "gy"), None),
        P(("gx", "gy")),
        P(None, ("gx", "gy")),
        P(None, ("gx", "gy")),
        P(("gx", "gy")),
    )
    return jax.shard_map(
        body,
        mesh=mesh,
        in_specs=placed,
        out_specs=(P(("gx", "gy"), None), P(("gx", "gy"))),
        check_vma=False,
    )
```

```python
import jax
import jax.numpy as jnp
from jax import lax
from jax.experimental import pallas as pl
from jax.experimental.pallas import tpu as pltpu
from jax.sharding import PartitionSpec as P

BS = 64
K = 7
RB = 8
NA = 2
AW = 640
HALF = 256
AGG = NA * BS
EDGE = 9 * BS + 8
SLOT = 5 * BS + 8
OMEGA = 2.0 / 3.0
F32 = jnp.float32
BF16 = jnp.bfloat16


def split(x):
    high = x.astype(BF16)
    return high, (x - high.astype(F32)).astype(BF16)


def dot3(a, b, side=1):
    def dot(x, y):
        return lax.dot_general(x, y, (((side,), (0,)), ((), ())), preferred_element_type=F32)

    return dot(a[0], b[0]) + (dot(a[0], b[1]) + dot(a[1], b[0]))


def lane_half(rows):
    return lax.broadcasted_iota(jnp.int32, (rows, 2 * BS), 1) // BS


def doubled(pair):
    low = lane_half(BS) == 0
    other = pltpu.roll(pair, BS, 1)
    return jnp.where(low, pair, other), jnp.where(low, other, pair)


def place(pairs, members):
    half = lane_half(BS)
    rows = []
    for p, pair in enumerate(pairs):
        for q, block in enumerate(doubled(pair)):
            rows.append(jnp.where(half == members[2 * p + q], block, 0.0))
    return jnp.concatenate(rows, 0)


def block_diagonal(low, high):
    tall = jnp.concatenate([jnp.concatenate([low, high], 1)] * 4, 0)
    row = lax.broadcasted_iota(jnp.int32, tall.shape, 0) // BS
    column = lax.broadcasted_iota(jnp.int32, tall.shape, 1) // BS
    return jnp.where(row == column, tall, 0.0)


def piece(ref, c):
    return ref[c * BS : (c + 1) * BS]


def received_members(ref):
    return [ref[9 * BS + m : 9 * BS + m + 1].astype(jnp.int32) for m in range(4)]


def received_place(ref):
    return place([piece(ref, 0), piece(ref, 1)], received_members(ref))


def frame_columns(frame, first, columns):
    return jnp.concatenate([frame[first : first + 4, c].reshape(HALF, 2 * BS) for c in columns], 1)


def frame_kernel(
    nbr_in,
    agg_in,
    blocks_in,
    tent_in,
    dinv_in,
    frame,
    tent,
    dinv,
    up,
    down,
    nbr,
    agg,
    blocks,
    sems,
):
    small = [
        pltpu.make_async_copy(nbr_in, nbr, sems.at[0]),
        pltpu.make_async_copy(agg_in, agg, sems.at[1]),
    ]
    rows = [pltpu.make_async_copy(blocks_in.at[i], blocks.at[i], sems.at[2 + i]) for i in range(RB)]
    others = [
        pltpu.make_async_copy(tent_in, tent, sems.at[2 + RB]),
        pltpu.make_async_copy(dinv_in, dinv, sems.at[3 + RB]),
    ]
    for copy in small + rows + others:
        copy.start()
    half = lane_half(BS)
    for i in range(RB):
        for c in range(6):
            frame[i, c] = jnp.zeros((BS, 2 * BS), F32)
    for copy in small:
        copy.wait()
    first = nbr[0, 0]
    for i in range(RB):
        rows[i].wait()
        origin = first - 4 if i < 4 else first
        mine = i + 4 if i < 4 else i
        copies = []
        for p in range(3):
            copies.extend(doubled(blocks[i, :, 2 * p * BS : 2 * (p + 1) * BS]))
        last = blocks[i, :, 6 * BS : 7 * BS]
        copies.append(jnp.concatenate([last, last], 1))
        frame[i, mine // 2] = jnp.where(half == mine % 2, copies[0], 0.0)
        for k in range(1, K):
            at = nbr[i, k] - origin
            column = at >> 1
            frame[i, column] = frame[i, column] + jnp.where(half == (at & 1), copies[k], 0.0)
    for copy in others:
        copy.wait()

    def send(out, pieces, members):
        for c, value in enumerate(pieces):
            out[c * BS : (c + 1) * BS] = value
        row = lax.broadcasted_iota(jnp.int32, (8, 2 * BS), 0)
        value = jnp.zeros((8, 2 * BS), F32)
        for m, member in enumerate(members):
            value = jnp.where(row == m, member.astype(F32), value)
        out[9 * BS :] = value

    owner = first // 4
    low = half == 0
    send(
        up,
        [tent[:, 256:384], tent[:, 384:512], dinv[:, 256:384], dinv[:, 384:512]]
        + [frame[7, 4], frame[7, 5], frame[6, 4]]
        + [jnp.where(low, frame[6, 5], pltpu.roll(frame[4, 4], BS, 1)), frame[5, 4]],
        [agg[4 + m] - owner for m in range(4)],
    )
    send(
        down,
        [tent[:, 0:128], tent[:, 128:256], dinv[:, 0:128], dinv[:, 128:256]]
        + [frame[0, 0], frame[0, 1]]
        + [jnp.where(low, pltpu.roll(frame[3, 1], BS, 1), frame[1, 0]), frame[1, 1], frame[2, 1]],
        [agg[m] - owner for m in range(4)],
    )


def own_kernel(frame, tent, dinv, up, down, a_high, a_low, near, factors, own, image):
    a = split(
        jnp.concatenate(
            [frame_columns(frame, 0, range(2, 6)), frame_columns(frame, 4, range(0, 4))], 0
        )
    )
    a_high[...], a_low[...] = a
    placed = place(
        [tent[:, 2 * p * BS : 2 * (p + 1) * BS] for p in range(4)],
        received_members(down) + received_members(up),
    )
    near[...] = placed
    summed = dot3(a, split(placed))
    parts = []
    for s, columns in ((0, (0, 1)), (1, (4, 5))):
        rows = slice(s * HALF, (s + 1) * HALF)
        inverse = split(
            block_diagonal(
                dinv[:, s * HALF : s * HALF + 128], dinv[:, s * HALF + 128 : (s + 1) * HALF]
            )
        )
        parts.append(placed[rows] - OMEGA * dot3(inverse, split(summed[rows])))
        factors[s] = -OMEGA * dot3(inverse, split(frame_columns(frame, 4 * s, columns)))
    prolong = jnp.concatenate(parts, 0)
    own[...] = prolong
    image[...] = dot3(a, split(prolong))


def edge_kernel(a_high, a_low, factors, own, image, below, above, side, left, right, up, down):
    b_low = dot3(split(factors[0]), split(received_place(below)))
    b_high = dot3(split(factors[1]), split(received_place(above)))
    side[:HALF] = b_low
    side[HALF:] = b_high
    b_low, b_high = split(b_low), split(b_high)
    image_left = dot3((a_high[:, :HALF], a_low[:, :HALF]), b_low)
    image_right = dot3((a_high[:, HALF:], a_low[:, HALF:]), b_high)
    left[...] = image_left
    right[...] = image_right
    for out, factor, rows in ((down, b_low, slice(0, HALF)), (up, b_high, slice(HALF, 2 * HALF))):
        terms = dot3(
            factor,
            split(jnp.concatenate([image_left[rows], image[rows], image_right[rows]], 1)),
            0,
        )
        for c in range(3):
            out[c * AGG : (c + 1) * AGG] = terms[:, c * AGG : (c + 1) * AGG]
        out[3 * AGG :] = own[rows]


def middle_kernel(frame, near, own, image, side, left, right, below, above, part, lo, hi, slots):
    own_low, own_high = own[:HALF], own[HALF:]
    c_low, c_high = split(own_low), split(own_high)
    middle = dot3(
        split(own[...]), split(jnp.concatenate([left[...], image[...], right[...]], 1)), 0
    )
    low = lane_half(BS) == 0
    none = jnp.zeros((BS, 2 * BS), F32)

    def square(rows):
        return split(jnp.concatenate([jnp.concatenate(row, 1) for row in rows], 0))

    seven = piece(below, 7)
    a_below = square(
        [
            [jnp.where(low, pltpu.roll(seven, BS, 1), 0.0), none],
            [piece(below, 8), none],
            [piece(below, 6), jnp.where(low, seven, 0.0)],
            [piece(below, 4), piece(below, 5)],
        ]
    )
    six = piece(above, 6)
    a_above = square(
        [
            [piece(above, 4), piece(above, 5)],
            [jnp.where(low, 0.0, six), piece(above, 7)],
            [none, piece(above, 8)],
            [none, jnp.where(low, 0.0, pltpu.roll(six, BS, 1))],
        ]
    )
    inverse = split(block_diagonal(piece(below, 2), piece(below, 3)))
    b_below = split(
        -OMEGA * dot3(inverse, split(dot3(a_below, split(near[:HALF]))))
    )
    inverse = split(block_diagonal(piece(above, 2), piece(above, 3)))
    b_above = split(
        -OMEGA * dot3(inverse, split(dot3(a_above, split(near[HALF:]))))
    )
    x_low = dot3(
        b_below, split(dot3(a_below, split(jnp.concatenate([side[:HALF], own_low], 1)))), 0
    )
    x_high = dot3(
        b_above, split(dot3(a_above, split(jnp.concatenate([own_high, side[HALF:]], 1)))), 0
    )
    t_low = dot3(c_low, split(frame_columns(frame, 0, (0, 1))), 0)
    t_high = dot3(c_high, split(frame_columns(frame, 4, (4, 5))), 0)
    lo[...] = t_low
    hi[...] = t_high
    part[:, :AGG] = middle[:, :AGG] + x_low[:, :AGG]
    part[:, AGG : 2 * AGG] = (
        middle[:, AGG : 2 * AGG]
        + (x_low[:, AGG:] + dot3(split(t_low), b_below))
        + (x_high[:, :AGG] + dot3(split(t_high), b_above))
    )
    part[:, 2 * AGG :] = middle[:, 2 * AGG :] + x_high[:, AGG:]
    for g in range(RB):
        slots[g] = jnp.zeros((SLOT, 2 * BS), F32)


def finish_kernel(nbr, target, part, lo, hi, below, above, empty, out):
    del empty
    first_id = nbr[0, 0] // 4
    band = [
        below[:AGG],
        part[:, :AGG]
        + below[AGG : 2 * AGG]
        + dot3(split(lo[...]), split(below[3 * AGG :])),
        part[:, AGG : 2 * AGG] + below[2 * AGG : 3 * AGG] + above[:AGG],
        part[:, 2 * AGG :]
        + above[AGG : 2 * AGG]
        + dot3(split(hi[...]), split(above[3 * AGG :])),
        above[2 * AGG : 3 * AGG],
    ]
    for u in range(NA):
        g = target[u]
        for c in range(5):
            out[g, c * BS : (c + 1) * BS] = band[c][u * BS : (u + 1) * BS]
        out[g, 5 * BS :] = jnp.full((8, 2 * BS), first_id + (u + 1), jnp.int32).astype(F32)


def unpack_kernel(got, rows, ids, sems):
    copies = [
        pltpu.make_async_copy(
            got.at[:, c * BS : (c + 1) * BS], rows.at[:, :, c * 128 : (c + 1) * 128], sems.at[c]
        )
        for c in range(5)
    ]
    for copy in copies:
        copy.start()
    lane = lax.broadcasted_iota(jnp.int32, (1, 2 * BS), 1)
    found = jnp.zeros((1, 2 * BS), F32)
    for s in range(RB):
        found = jnp.where(lane == s, got[s, 5 * BS : 5 * BS + 1], found)
    ids[...] = (found.astype(jnp.int32) - 1)[0, :RB]
    for copy in copies:
        copy.wait()


VMEM = pl.BlockSpec(memory_space=pltpu.VMEM)
SMEM = pl.BlockSpec(memory_space=pltpu.SMEM)
HBM = pl.BlockSpec(memory_space=pltpu.HBM)


def call(kernel, ins, outs, scratch=(), aliases=None):
    return pl.pallas_call(
        kernel,
        in_specs=[memory for memory, _ in ins],
        out_specs=[memory for memory, _, _ in outs],
        out_shape=[jax.ShapeDtypeStruct(shape, dtype) for _, shape, dtype in outs],
        scratch_shapes=list(scratch),
        input_output_aliases=aliases or {},
        compiler_params=pltpu.CompilerParams(vmem_limit_bytes=32 * 1024 * 1024),
        name=kernel.__name__,
    )(*[array for _, array in ins])


def on_chip(*arrays):
    return [(VMEM, array) for array in arrays]


def body(blocks, neighbors, aggregate, tentative, inv_diagonal, target):
    axes = ("gx", "gy")
    devices = lax.axis_size(axes)
    upward = [(i, i + 1) for i in range(devices - 1)]
    downward = [(j, i) for i, j in upward]
    frame, tent, dinv, up, down = call(
        frame_kernel,
        [(HBM, pltpu.with_memory_space_constraint(x, pltpu.HBM)) for x in (neighbors, aggregate, blocks, tentative, inv_diagonal)],
        [
            (VMEM, (RB, 6, BS, 2 * BS), F32),
            (VMEM, (BS, RB * BS), F32),
            (VMEM, (BS, RB * BS), F32),
            (VMEM, (EDGE, 2 * BS), F32),
            (VMEM, (EDGE, 2 * BS), F32),
        ],
        [
            pltpu.SMEM((RB, K), jnp.int32),
            pltpu.SMEM((RB,), jnp.int32),
            pltpu.VMEM((RB, BS, K * BS), F32),
            pltpu.SemaphoreType.DMA((4 + RB,)),
        ],
    )
    below = lax.ppermute(up, axes, upward)
    above = lax.ppermute(down, axes, downward)
    tall = (VMEM, (2 * HALF, AGG), F32)
    a_high, a_low, near, factors, own, image = call(
        own_kernel,
        on_chip(frame, tent, dinv, up, down),
        [
            (VMEM, (2 * HALF, 2 * HALF), BF16),
            (VMEM, (2 * HALF, 2 * HALF), BF16),
            tall,
            (VMEM, (2, HALF, HALF), F32),
            tall,
            tall,
        ],
    )
    side, left, right, up, down = call(
        edge_kernel,
        on_chip(a_high, a_low, factors, own, image, below, above),
        [tall] * 3 + [(VMEM, (5 * AGG, AGG), F32)] * 2,
    )
    below_terms = lax.ppermute(up, axes, upward)
    above_terms = lax.ppermute(down, axes, downward)
    slots_out = (VMEM, (RB, SLOT, 2 * BS), F32)
    part, lo, hi, slots = call(
        middle_kernel,
        on_chip(frame, near, own, image, side, left, right, below, above),
        [
            (VMEM, (AGG, 3 * AGG), F32),
            (VMEM, (AGG, HALF), F32),
            (VMEM, (AGG, HALF), F32),
            slots_out,
        ],
    )
    (slots,) = call(
        finish_kernel,
        [(SMEM, neighbors), (SMEM, target)]
        + on_chip(part, lo, hi, below_terms, above_terms, slots),
        [slots_out],
        aliases={7: 0},
    )
    got = lax.all_to_all(slots, "gy", split_axis=0, concat_axis=0, tiled=True)
    rows, ids = call(
        unpack_kernel,
        on_chip(got),
        [(HBM, (RB, BS, AW), F32), (VMEM, (RB,), jnp.int32)],
        [pltpu.SemaphoreType.DMA((5,))],
    )
    return rows.reshape(RB * BS, AW), ids


def solution(mesh):
    placed = (
        P(("gx", "gy"), None, None),
        P(("gx", "gy"), None),
        P(("gx", "gy")),
        P(None, ("gx", "gy")),
        P(None, ("gx", "gy")),
        P(("gx", "gy")),
    )
    return jax.shard_map(
        body,
        mesh=mesh,
        in_specs=placed,
        out_specs=(P(("gx", "gy"), None), P(("gx", "gy"))),
        check_vma=False,
    )
```

```python
import jax
import jax.numpy as jnp
from jax import lax
from jax.experimental import pallas as pl
from jax.experimental.pallas import tpu as pltpu
from jax.sharding import PartitionSpec as P

BS = 64
K = 7
RB = 8
NA = 2
AW = 640
HALF = 256
AGG = NA * BS
UP = 9 * BS + 8 + HALF
DOWN = 2 * BS + 8
SLOT = 5 * BS // 8 + 1
OMEGA = 2.0 / 3.0
F32 = jnp.float32
BF16 = jnp.bfloat16


def split(x):
    high = x.astype(BF16)
    return high, (x - high.astype(F32)).astype(BF16)


def dot3(a, b, side=1):
    def dot(x, y):
        return lax.dot_general(x, y, (((side,), (0,)), ((), ())), preferred_element_type=F32)

    return dot(a[0], b[0]) + (dot(a[0], b[1]) + dot(a[1], b[0]))


def lane_half(rows):
    return lax.broadcasted_iota(jnp.int32, (rows, 2 * BS), 1) // BS


def doubled(pair):
    low = lane_half(BS) == 0
    other = pltpu.roll(pair, BS, 1)
    return jnp.where(low, pair, other), jnp.where(low, other, pair)


def place(pairs, members):
    half = lane_half(BS)
    rows = []
    for p, pair in enumerate(pairs):
        for q, block in enumerate(doubled(pair)):
            rows.append(jnp.where(half == members[2 * p + q], block, 0.0))
    return jnp.concatenate(rows, 0)


def block_diagonal(low, high):
    tall = jnp.concatenate([jnp.concatenate([low, high], 1)] * 4, 0)
    row = lax.broadcasted_iota(jnp.int32, tall.shape, 0) // BS
    column = lax.broadcasted_iota(jnp.int32, tall.shape, 1) // BS
    return jnp.where(row == column, tall, 0.0)


def piece(ref, c):
    return ref[c * BS : (c + 1) * BS]


def received_place(ref, members):
    rows = [ref[members + m : members + m + 1].astype(jnp.int32) for m in range(4)]
    return place([piece(ref, 0), piece(ref, 1)], rows)


def frame_columns(frame, first, columns):
    return jnp.concatenate([frame[first : first + 4, c].reshape(HALF, 2 * BS) for c in columns], 1)


def doubled_row(blocks, i):
    copies = []
    for p in range(3):
        copies.extend(doubled(blocks[i, :, 2 * p * BS : 2 * (p + 1) * BS]))
    last = blocks[i, :, 6 * BS : 7 * BS]
    return copies + [jnp.concatenate([last, last], 1)]


def own_prolong(own_rows, near, inverse, rows):
    summed = dot3(own_rows, split(near))
    return near[rows] - OMEGA * dot3(inverse, split(summed))


def frame_kernel(
    nbr_in, agg_in, blocks_in, tent_in, dinv_in, frame, dinv, near, odd, up, down, nbr, agg, blocks, tent, sems
):
    small = [
        pltpu.make_async_copy(nbr_in, nbr, sems.at[0]),
        pltpu.make_async_copy(agg_in, agg, sems.at[1]),
    ]
    rows = [pltpu.make_async_copy(blocks_in.at[i], blocks.at[i], sems.at[2 + i]) for i in range(RB)]
    others = [
        pltpu.make_async_copy(tent_in, tent, sems.at[2 + RB]),
        pltpu.make_async_copy(dinv_in, dinv, sems.at[3 + RB]),
    ]
    for copy in small + others + rows:
        copy.start()
    half = lane_half(BS)
    for i in range(RB):
        for c in range(6):
            frame[i, c] = jnp.zeros((BS, 2 * BS), F32)
    for copy in small + others:
        copy.wait()
    first = nbr[0, 0]
    owner = first // 4
    odd[...] = jnp.full((8, 2 * BS), (first // RB) & 1, jnp.int32)
    near[...] = place(
        [tent[:, 2 * p * BS : 2 * (p + 1) * BS] for p in range(4)],
        [agg[j] - owner for j in range(RB)],
    )
    for i in range(RB):
        rows[i].wait()
        origin = first - 4 if i < 4 else first
        mine = i + 4 if i < 4 else i
        copies = doubled_row(blocks, i)
        frame[i, mine // 2] = jnp.where(half == mine % 2, copies[0], 0.0)
        for k in range(1, K):
            at = nbr[i, k] - origin
            column = at >> 1
            frame[i, column] = frame[i, column] + jnp.where(half == (at & 1), copies[k], 0.0)

    def send(out, pieces, members):
        for c, value in enumerate(pieces):
            out[c * BS : (c + 1) * BS] = value
        row = lax.broadcasted_iota(jnp.int32, (8, 2 * BS), 0)
        value = jnp.zeros((8, 2 * BS), F32)
        for m, member in enumerate(members):
            value = jnp.where(row == m, member.astype(F32), value)
        out[len(pieces) * BS : len(pieces) * BS + 8] = value

    low = half == 0
    send(
        up,
        [tent[:, 256:384], tent[:, 384:512], dinv[:, 256:384], dinv[:, 384:512]]
        + [frame[7, 4], frame[7, 5], frame[6, 4]]
        + [jnp.where(low, frame[6, 5], pltpu.roll(frame[4, 4], BS, 1)), frame[5, 4]],
        [agg[4 + m] - owner for m in range(4)],
    )
    send(down, [tent[:, 0:128], tent[:, 128:256]], [agg[m] - owner for m in range(4)])
    up[UP - HALF :] = own_prolong(
        split(frame_columns(frame, 4, range(0, 4))),
        near[...],
        split(block_diagonal(dinv[:, 256:384], dinv[:, 384:512])),
        slice(HALF, 2 * HALF),
    )


def own_kernel(
    frame, dinv, near, up, a_high, a_low, factors, inner, outer, cross, crossed, own, image
):
    lower = split(frame_columns(frame, 0, range(2, 6)))
    upper = split(frame_columns(frame, 4, range(0, 4)))
    a = [jnp.concatenate([x, y], 0) for x, y in zip(lower, upper)]
    a_high[...], a_low[...] = a
    inverse = [
        split(block_diagonal(dinv[:, s * HALF : s * HALF + 128], dinv[:, s * HALF + 128 : (s + 1) * HALF]))
        for s in range(2)
    ]
    c_low = own_prolong(lower, near[...], inverse[0], slice(0, HALF))
    edge = [split(frame_columns(frame, 0, (0, 1))), split(frame_columns(frame, 4, (4, 5)))]
    both = []
    for s in range(2):
        factor = -OMEGA * dot3(inverse[s], edge[s])
        factors[s] = factor
        both.append(split(factor))
    prolong = jnp.concatenate([c_low, up[UP - HALF :]], 0)
    own[...] = prolong
    applied = dot3(a, split(prolong))
    image[...] = applied
    for t in range(2):
        columns = slice(t * HALF, (t + 1) * HALF)
        moved = dot3((a[0][:, columns], a[1][:, columns]), both[t])
        for s in range(2):
            inner[s, t] = dot3(both[s], split(moved[s * HALF : (s + 1) * HALF]), 0)
    for s in range(2):
        outer[s] = dot3(both[s], split(applied[s * HALF : (s + 1) * HALF]), 0)
    cross[...] = dot3(both[0], edge[0], 0)
    crossed[...] = dot3(split(c_low), edge[0], 0)


def edge_kernel(
    odd, inner, outer, cross, factors, near, own, below, above, side, far, moved, early, late
):
    placed = [split(received_place(below, 9 * BS)), split(received_place(above, 2 * BS))]
    low = lane_half(BS) == 0
    none = jnp.zeros((BS, 2 * BS), F32)
    seven = piece(below, 7)
    a_below = split(
        jnp.concatenate(
            [
                jnp.concatenate(row, 1)
                for row in [
                    [jnp.where(low, pltpu.roll(seven, BS, 1), 0.0), none],
                    [piece(below, 8), none],
                    [piece(below, 6), jnp.where(low, seven, 0.0)],
                    [piece(below, 4), piece(below, 5)],
                ]
            ],
            0,
        )
    )
    inverse = split(block_diagonal(piece(below, 2), piece(below, 3)))
    b_below = -OMEGA * dot3(inverse, split(dot3(a_below, split(near[:HALF]))))
    b_low = dot3(split(factors[0]), placed[0])
    image_low = dot3(a_below, split(jnp.concatenate([b_low, own[:HALF]], 1)))
    c_below = below[UP - HALF :]
    far_rows = jnp.concatenate([c_below, b_below], 1)
    side[...] = b_low
    far[...] = far_rows
    moved[...] = image_low
    across = dot3(split(cross[...]), split(far_rows))
    terms = []
    for s in range(2):
        left, right = [dot3(split(inner[s, t]), placed[t]) for t in range(2)]
        middle = outer[s]
        if s == 0:
            left = left + across[:, :AGG]
            middle = middle + across[:, AGG:]
        terms.append(dot3(placed[s], split(jnp.concatenate([left, middle, right], 1)), 0))
    lower_terms = dot3(split(c_below), split(image_low), 0)
    upward = odd[:1] == 1
    for c in range(3):
        columns = slice(c * AGG, (c + 1) * AGG)
        down, up = terms[0][:, columns], terms[1][:, columns]
        if c < 2:
            down = down + lower_terms[:, columns]
        early[columns] = jnp.where(upward, up, down)
        late[columns] = jnp.where(upward, down, up)


def middle_kernel(
    a_high, a_low, factors, crossed, own, image, above, side, far, moved, part, slots
):
    b_high = dot3(split(factors[1]), split(received_place(above, 2 * BS)))
    left = dot3((a_high[:, :HALF], a_low[:, :HALF]), split(side[...]))
    right = dot3((a_high[:, HALF:], a_low[:, HALF:]), split(b_high))
    middle = dot3(split(own[...]), split(jnp.concatenate([left, image[...], right], 1)), 0)
    lower = dot3(split(far[:, AGG:]), split(moved[...]), 0) + dot3(
        split(crossed[...]), split(far[...])
    )
    part[:, : 2 * AGG] = middle[:, : 2 * AGG] + lower
    part[:, 2 * AGG :] = middle[:, 2 * AGG :]
    for g in range(RB):
        slots[g] = jnp.zeros((SLOT, 8, 2 * BS), F32)


def finish_kernel(nbr, target, odd, part, early, late, empty, out):
    del empty
    first_id = nbr[0, 0] // 4
    upward = odd[:1] == 1
    below = [
        jnp.where(upward, late[c * AGG : (c + 1) * AGG], early[c * AGG : (c + 1) * AGG])
        for c in range(3)
    ]
    above = [
        jnp.where(upward, early[c * AGG : (c + 1) * AGG], late[c * AGG : (c + 1) * AGG])
        for c in range(3)
    ]
    band = [
        below[0],
        part[:, :AGG] + below[1],
        part[:, AGG : 2 * AGG] + below[2] + above[0],
        part[:, 2 * AGG :] + above[1],
        above[2],
    ]
    for u in range(NA):
        g = target[u]
        for r in range(8):
            for c in range(5):
                out[g, 5 * r + c] = band[c][u * BS + 8 * r : u * BS + 8 * (r + 1)]
        out[g, SLOT - 1] = jnp.full((8, 2 * BS), first_id + (u + 1), jnp.int32).astype(F32)


def unpack_kernel(got, rows, ids, sem):
    copy = pltpu.make_async_copy(got.at[:, : SLOT - 1], rows, sem)
    copy.start()
    lane = lax.broadcasted_iota(jnp.int32, (1, 2 * BS), 1)
    found = jnp.zeros((1, 2 * BS), F32)
    for s in range(RB):
        found = jnp.where(lane == s, got[s, SLOT - 1, :1], found)
    ids[...] = (found.astype(jnp.int32) - 1)[0, :RB]
    copy.wait()


VMEM = pl.BlockSpec(memory_space=pltpu.VMEM)
SMEM = pl.BlockSpec(memory_space=pltpu.SMEM)
HBM = pl.BlockSpec(memory_space=pltpu.HBM)


def call(kernel, ins, outs, scratch=(), aliases=None):
    return pl.pallas_call(
        kernel,
        in_specs=[memory for memory, _ in ins],
        out_specs=[memory for memory, _, _ in outs],
        out_shape=[jax.ShapeDtypeStruct(shape, dtype) for _, shape, dtype in outs],
        scratch_shapes=list(scratch),
        input_output_aliases=aliases or {},
        compiler_params=pltpu.CompilerParams(vmem_limit_bytes=32 * 1024 * 1024),
        name=kernel.__name__,
    )(*[array for _, array in ins])


def on_chip(*arrays):
    return [(VMEM, array) for array in arrays]


def body(blocks, neighbors, aggregate, tentative, inv_diagonal, target):
    axes = ("gx", "gy")
    devices = lax.axis_size(axes)
    upward = [(i, i + 1) for i in range(devices - 1)]
    downward = [(j, i) for i, j in upward]
    tall = (VMEM, (2 * HALF, AGG), F32)
    square = (VMEM, (HALF, HALF), F32)
    frame, dinv, near, odd, up, down = call(
        frame_kernel,
        [
            (HBM, pltpu.with_memory_space_constraint(x, pltpu.HBM))
            for x in (neighbors, aggregate, blocks, tentative, inv_diagonal)
        ],
        [
            (VMEM, (RB, 6, BS, 2 * BS), F32),
            (VMEM, (BS, RB * BS), F32),
            tall,
            (VMEM, (8, 2 * BS), jnp.int32),
            (VMEM, (UP, 2 * BS), F32),
            (VMEM, (DOWN, 2 * BS), F32),
        ],
        [
            pltpu.SMEM((RB, K), jnp.int32),
            pltpu.SMEM((RB,), jnp.int32),
            pltpu.VMEM((RB, BS, K * BS), F32),
            pltpu.VMEM((BS, RB * BS), F32),
            pltpu.SemaphoreType.DMA((4 + RB,)),
        ],
    )
    below = lax.ppermute(up, axes, upward)
    above = lax.ppermute(down, axes, downward)
    a_high, a_low, factors, inner, outer, cross, crossed, own, image = call(
        own_kernel,
        on_chip(frame, dinv, near, up),
        [
            (VMEM, (2 * HALF, 2 * HALF), BF16),
            (VMEM, (2 * HALF, 2 * HALF), BF16),
            (VMEM, (2, HALF, HALF), F32),
            (VMEM, (2, 2, HALF, HALF), F32),
            (VMEM, (2, HALF, AGG), F32),
            square,
            (VMEM, (AGG, HALF), F32),
            tall,
            tall,
        ],
    )
    side, far, moved, early, late = call(
        edge_kernel,
        on_chip(odd, inner, outer, cross, factors, near, own, below, above),
        [(VMEM, (HALF, AGG), F32), square, square] + [(VMEM, (3 * AGG, AGG), F32)] * 2,
    )
    odd_pairs = [(i, i + 1 if i % 2 else i - 1) for i in range(1, devices - 1)]
    even_pairs = [(i, i ^ 1) for i in range(devices)]
    early = lax.ppermute(early, axes, odd_pairs)
    late = lax.ppermute(late, axes, even_pairs)
    slots_out = (VMEM, (RB, SLOT, 8, 2 * BS), F32)
    part, slots = call(
        middle_kernel,
        on_chip(a_high, a_low, factors, crossed, own, image, above, side, far, moved),
        [(VMEM, (AGG, 3 * AGG), F32), slots_out],
    )
    (slots,) = call(
        finish_kernel,
        [(SMEM, neighbors), (SMEM, target)] + on_chip(odd, part, early, late, slots),
        [slots_out],
        aliases={6: 0},
    )
    got = lax.all_to_all(slots, "gy", split_axis=0, concat_axis=0, tiled=True)
    tiles, ids = call(
        unpack_kernel,
        on_chip(got),
        [(HBM, (RB, SLOT - 1, 8, 2 * BS), F32), (VMEM, (RB,), jnp.int32)],
        [pltpu.SemaphoreType.DMA(())],
    )
    rows = tiles.reshape(RB * BS // 8, AW // 128, 8, 128).transpose(0, 2, 1, 3)
    return rows.reshape(RB * BS, AW), ids


def solution(mesh):
    placed = (
        P(("gx", "gy"), None, None),
        P(("gx", "gy"), None),
        P(("gx", "gy")),
        P(None, ("gx", "gy")),
        P(None, ("gx", "gy")),
        P(("gx", "gy")),
    )
    return jax.shard_map(
        body,
        mesh=mesh,
        in_specs=placed,
        out_specs=(P(("gx", "gy"), None), P(("gx", "gy"))),
        check_vma=False,
    )
```

```python
import jax
import jax.numpy as jnp
from jax import lax
from jax.experimental import pallas as pl
from jax.experimental.pallas import tpu as pltpu
from jax.sharding import PartitionSpec as P

BS = 64
K = 7
RB = 8
NA = 2
AW = 640
HALF = 256
AGG = NA * BS
UP = 9 * BS + 8 + HALF
DOWN = 2 * BS + 8
SLOT = 5 * BS // 8 + 1
OMEGA = 2.0 / 3.0
F32 = jnp.float32
BF16 = jnp.bfloat16


def split(x):
    high = x.astype(BF16)
    return high, (x - high.astype(F32)).astype(BF16)


def dot3(a, b, side=1):
    def dot(x, y):
        return lax.dot_general(x, y, (((side,), (0,)), ((), ())), preferred_element_type=F32)

    return dot(a[0], b[0]) + (dot(a[0], b[1]) + dot(a[1], b[0]))


def lane_half(rows):
    return lax.broadcasted_iota(jnp.int32, (rows, 2 * BS), 1) // BS


def doubled(pair):
    low = lane_half(BS) == 0
    other = pltpu.roll(pair, BS, 1)
    return jnp.where(low, pair, other), jnp.where(low, other, pair)


def place(pairs, members):
    half = lane_half(BS)
    rows = []
    for p, pair in enumerate(pairs):
        for q, block in enumerate(doubled(pair)):
            rows.append(jnp.where(half == members[2 * p + q], block, 0.0))
    return jnp.concatenate(rows, 0)


def block_diagonal(low, high):
    tall = jnp.concatenate([jnp.concatenate([low, high], 1)] * 4, 0)
    row = lax.broadcasted_iota(jnp.int32, tall.shape, 0) // BS
    column = lax.broadcasted_iota(jnp.int32, tall.shape, 1) // BS
    return jnp.where(row == column, tall, 0.0)


def piece(ref, c):
    return ref[c * BS : (c + 1) * BS]


def received_place(ref, members):
    rows = [ref[members + m : members + m + 1].astype(jnp.int32) for m in range(4)]
    return place([piece(ref, 0), piece(ref, 1)], rows)


def frame_columns(frame, columns):
    return jnp.concatenate([frame[:, c].reshape(HALF, 2 * BS) for c in columns], 1)


def doubled_row(blocks, i):
    copies = []
    for p in range(3):
        copies.extend(doubled(blocks[i, :, 2 * p * BS : 2 * (p + 1) * BS]))
    last = blocks[i, :, 6 * BS : 7 * BS]
    return copies + [jnp.concatenate([last, last], 1)]


def own_prolong(own_rows, near, inverse, rows):
    summed = dot3(own_rows, split(near))
    return near[rows] - OMEGA * dot3(inverse, split(summed))


def spread(nbr, blocks, frame, i, origin):
    half = lane_half(BS)
    row, mine = i % 4, i + 4 if i < 4 else i
    copies = doubled_row(blocks, row)
    for c in range(6):
        frame[row, c] = jnp.zeros((BS, 2 * BS), F32)
    frame[row, mine // 2] = jnp.where(half == mine % 2, copies[0], 0.0)
    for k in range(1, K):
        at = nbr[i, k] - origin
        column = at >> 1
        frame[row, column] = frame[row, column] + jnp.where(half == (at & 1), copies[k], 0.0)


def frame_kernel(
    nbr_in, agg_in, blocks_in, tent_in, dinv_in, frame, near, odd, up, down, nbr, agg, blocks, sems
):
    def pieces(source, first, out, at, sem):
        return [
            pltpu.make_async_copy(
                source.at[:, first + c * 128 : first + (c + 1) * 128],
                out.at[at + c * BS : at + (c + 1) * BS],
                sems.at[sem + c],
            )
            for c in range(2)
        ]

    small = [
        pltpu.make_async_copy(nbr_in, nbr, sems.at[0]),
        pltpu.make_async_copy(agg_in, agg, sems.at[1]),
    ]
    tents = pieces(tent_in, 0, down, 0, 2) + pieces(tent_in, HALF, up, 0, 4)
    dinvs = pieces(dinv_in, HALF, up, 2 * BS, 6)
    rows = [
        pltpu.make_async_copy(blocks_in.at[4 + i], blocks.at[i], sems.at[8 + i]) for i in range(4)
    ]
    for copy in small + tents + rows + dinvs:
        copy.start()
    for copy in small + tents:
        copy.wait()
    first = nbr[0, 0]
    members = [agg[j] - first // 4 for j in range(RB)]
    odd[...] = jnp.full((8, 2 * BS), (first // RB) & 1, jnp.int32)
    near[...] = place([piece(ref, c) for ref in (down, up) for c in range(2)], members)
    row = lax.broadcasted_iota(jnp.int32, (8, 2 * BS), 0)
    for out, at, mine in ((down, 2 * BS, members[:4]), (up, 9 * BS, members[4:])):
        value = jnp.zeros((8, 2 * BS), F32)
        for m, member in enumerate(mine):
            value = jnp.where(row == m, member.astype(F32), value)
        out[at : at + 8] = value
    for i in range(4):
        rows[i].wait()
        spread(nbr, blocks, frame, 4 + i, first)
    for copy in dinvs:
        copy.wait()
    low = lane_half(BS) == 0
    for c, value in enumerate(
        [frame[3, 4], frame[3, 5], frame[2, 4]]
        + [jnp.where(low, frame[2, 5], pltpu.roll(frame[0, 4], BS, 1)), frame[1, 4]]
    ):
        up[(4 + c) * BS : (5 + c) * BS] = value
    up[UP - HALF :] = own_prolong(
        split(frame_columns(frame, range(0, 4))),
        near[...],
        split(block_diagonal(piece(up, 2), piece(up, 3))),
        slice(HALF, 2 * HALF),
    )


def own_kernel(
    nbr_in,
    blocks_in,
    dinv_in,
    frame,
    near,
    up,
    a_high,
    a_low,
    factors,
    inner,
    outer,
    cross,
    crossed,
    own,
    image,
    nbr,
    blocks,
    dinv,
    low_frame,
    sems,
):
    copies = [
        pltpu.make_async_copy(nbr_in, nbr, sems.at[0]),
        pltpu.make_async_copy(blocks_in.at[:4], blocks, sems.at[1]),
        pltpu.make_async_copy(dinv_in.at[:, :HALF], dinv, sems.at[2]),
    ]
    for copy in copies:
        copy.start()
    upper = split(frame_columns(frame, range(0, 4)))
    inverse = [None, split(block_diagonal(piece(up, 2), piece(up, 3)))]
    edge = [None, split(frame_columns(frame, (4, 5)))]
    for copy in copies:
        copy.wait()
    for i in range(4):
        spread(nbr, blocks, low_frame, i, nbr[0, 0] - 4)
    lower = split(frame_columns(low_frame, range(2, 6)))
    inverse[0] = split(block_diagonal(dinv[:, :128], dinv[:, 128:]))
    edge[0] = split(frame_columns(low_frame, (0, 1)))
    a = [jnp.concatenate([x, y], 0) for x, y in zip(lower, upper)]
    a_high[...], a_low[...] = a
    c_low = own_prolong(lower, near[...], inverse[0], slice(0, HALF))
    both = []
    for s in range(2):
        factor = -OMEGA * dot3(inverse[s], edge[s])
        factors[s] = factor
        both.append(split(factor))
    prolong = jnp.concatenate([c_low, up[UP - HALF :]], 0)
    own[...] = prolong
    applied = dot3(a, split(prolong))
    image[...] = applied
    for t in range(2):
        columns = slice(t * HALF, (t + 1) * HALF)
        moved = dot3((a[0][:, columns], a[1][:, columns]), both[t])
        for s in range(2):
            inner[s, t] = dot3(both[s], split(moved[s * HALF : (s + 1) * HALF]), 0)
    for s in range(2):
        outer[s] = dot3(both[s], split(applied[s * HALF : (s + 1) * HALF]), 0)
    cross[...] = dot3(both[0], edge[0], 0)
    crossed[...] = dot3(split(c_low), edge[0], 0)


def edge_kernel(
    odd, inner, outer, cross, factors, near, own, below, above, side, far, moved, early, late
):
    placed = [split(received_place(below, 9 * BS)), split(received_place(above, 2 * BS))]
    low = lane_half(BS) == 0
    none = jnp.zeros((BS, 2 * BS), F32)
    seven = piece(below, 7)
    a_below = split(
        jnp.concatenate(
            [
                jnp.concatenate(row, 1)
                for row in [
                    [jnp.where(low, pltpu.roll(seven, BS, 1), 0.0), none],
                    [piece(below, 8), none],
                    [piece(below, 6), jnp.where(low, seven, 0.0)],
                    [piece(below, 4), piece(below, 5)],
                ]
            ],
            0,
        )
    )
    inverse = split(block_diagonal(piece(below, 2), piece(below, 3)))
    b_below = -OMEGA * dot3(inverse, split(dot3(a_below, split(near[:HALF]))))
    b_low = dot3(split(factors[0]), placed[0])
    image_low = dot3(a_below, split(jnp.concatenate([b_low, own[:HALF]], 1)))
    c_below = below[UP - HALF :]
    far_rows = jnp.concatenate([c_below, b_below], 1)
    side[...] = b_low
    far[...] = far_rows
    moved[...] = image_low
    across = dot3(split(cross[...]), split(far_rows))
    terms = []
    for s in range(2):
        left, right = [dot3(split(inner[s, t]), placed[t]) for t in range(2)]
        middle = outer[s]
        if s == 0:
            left = left + across[:, :AGG]
            middle = middle + across[:, AGG:]
        terms.append(dot3(placed[s], split(jnp.concatenate([left, middle, right], 1)), 0))
    lower_terms = dot3(split(c_below), split(image_low), 0)
    upward = odd[:1] == 1
    for c in range(3):
        columns = slice(c * AGG, (c + 1) * AGG)
        down, up = terms[0][:, columns], terms[1][:, columns]
        if c < 2:
            down = down + lower_terms[:, columns]
        early[columns] = jnp.where(upward, up, down)
        late[columns] = jnp.where(upward, down, up)


def middle_kernel(
    a_high, a_low, factors, crossed, own, image, above, side, far, moved, part
):
    b_high = dot3(split(factors[1]), split(received_place(above, 2 * BS)))
    left = dot3((a_high[:, :HALF], a_low[:, :HALF]), split(side[...]))
    right = dot3((a_high[:, HALF:], a_low[:, HALF:]), split(b_high))
    middle = dot3(split(own[...]), split(jnp.concatenate([left, image[...], right], 1)), 0)
    lower = dot3(split(far[:, AGG:]), split(moved[...]), 0) + dot3(
        split(crossed[...]), split(far[...])
    )
    part[:, : 2 * AGG] = middle[:, : 2 * AGG] + lower
    part[:, 2 * AGG :] = middle[:, 2 * AGG :]


def finish_kernel(nbr, target, odd, part, early, late, *outs):
    first_id = nbr[0, 0] // 4
    here = (nbr[0, 0] // RB) % RB
    upward = odd[:1] == 1
    below = [
        jnp.where(upward, late[c * AGG : (c + 1) * AGG], early[c * AGG : (c + 1) * AGG])
        for c in range(3)
    ]
    above = [
        jnp.where(upward, early[c * AGG : (c + 1) * AGG], late[c * AGG : (c + 1) * AGG])
        for c in range(3)
    ]
    band = [
        below[0],
        part[:, :AGG] + below[1],
        part[:, AGG : 2 * AGG] + below[2] + above[0],
        part[:, 2 * AGG :] + above[1],
        above[2],
    ]
    numbers = [jnp.full((8, 2 * BS), first_id + (u + 1), jnp.int32).astype(F32) for u in range(NA)]
    shifts = [(target[u] - here) & (RB - 1) for u in range(NA)]
    for shift, out in enumerate(outs):
        used = [jnp.full((8, 2 * BS), shifts[u], jnp.int32) == shift for u in range(NA)]

        def chosen(first, second):
            return jnp.where(used[0], first, jnp.where(used[1], second, 0.0))

        for r in range(8):
            for c in range(5):
                out[5 * r + c] = chosen(
                    *[band[c][u * BS + 8 * r : u * BS + 8 * (r + 1)] for u in range(NA)]
                )
        out[SLOT - 1] = chosen(*numbers)


def unpack(got, shifts, rows, sems, found):
    here = lax.axis_index("gy")
    copies = []
    sources = [(here - shift) & (RB - 1) for shift in shifts]
    for k, (source, ref) in enumerate(zip(sources, got)):
        copies.append(pltpu.make_async_copy(ref.at[: SLOT - 1], rows.at[source], sems.at[k]))
        copies[-1].start()
    lane = lax.broadcasted_iota(jnp.int32, (1, 2 * BS), 1)
    for source, ref in zip(sources, got):
        found = jnp.where(lane == source, ref[SLOT - 1, :1], found)
    return copies, found


def unpack_first_kernel(*refs):
    got, (rows, found, sems) = refs[: len(EARLY)], refs[len(EARLY) :]
    copies, numbers = unpack(got, EARLY, rows, sems, jnp.zeros((1, 2 * BS), F32))
    found[...] = numbers
    for copy in copies:
        copy.wait()


def unpack_second_kernel(begun, found, *refs):
    del begun
    got, (rows, ids, numbers, sems) = refs[: len(LATE)], refs[len(LATE) :]
    copies, held = unpack(got, LATE, rows, sems, found[...])
    numbers[...] = (held.astype(jnp.int32) - 1)[0, :RB]
    copies.append(pltpu.make_async_copy(numbers, ids, sems.at[len(LATE)]))
    copies[-1].start()
    for copy in copies:
        copy.wait()


SHIFTS = (4, 3, 5, 2, 6, 1, 7)
EARLY = (0,) + SHIFTS[:5]
LATE = SHIFTS[5:]


VMEM = pl.BlockSpec(memory_space=pltpu.VMEM)
SMEM = pl.BlockSpec(memory_space=pltpu.SMEM)
HBM = pl.BlockSpec(memory_space=pltpu.HBM)


def call(kernel, ins, outs, scratch=(), aliases=None):
    return pl.pallas_call(
        kernel,
        in_specs=[memory for memory, _ in ins],
        out_specs=[memory for memory, _, _ in outs],
        out_shape=[jax.ShapeDtypeStruct(shape, dtype) for _, shape, dtype in outs],
        scratch_shapes=list(scratch),
        input_output_aliases=aliases or {},
        compiler_params=pltpu.CompilerParams(vmem_limit_bytes=32 * 1024 * 1024),
        name=kernel.__name__,
    )(*[array for _, array in ins])


def on_chip(*arrays):
    return [(VMEM, array) for array in arrays]


def body(blocks, neighbors, aggregate, tentative, inv_diagonal, target):
    axes = ("gx", "gy")
    devices = lax.axis_size(axes)
    upward = [(i, i + 1) for i in range(devices - 1)]
    downward = [(j, i) for i, j in upward]
    tall = (VMEM, (2 * HALF, AGG), F32)
    square = (VMEM, (HALF, HALF), F32)
    pinned = [
        (HBM, pltpu.with_memory_space_constraint(x, pltpu.HBM))
        for x in (neighbors, aggregate, blocks, tentative, inv_diagonal)
    ]
    frame, near, odd, up, down = call(
        frame_kernel,
        pinned,
        [
            (VMEM, (4, 6, BS, 2 * BS), F32),
            tall,
            (VMEM, (8, 2 * BS), jnp.int32),
            (VMEM, (UP, 2 * BS), F32),
            (VMEM, (DOWN, 2 * BS), F32),
        ],
        [
            pltpu.SMEM((RB, K), jnp.int32),
            pltpu.SMEM((RB,), jnp.int32),
            pltpu.VMEM((4, BS, K * BS), F32),
            pltpu.SemaphoreType.DMA((12,)),
        ],
    )
    below = lax.ppermute(up, axes, upward)
    above = lax.ppermute(down, axes, downward)
    a_high, a_low, factors, inner, outer, cross, crossed, own, image = call(
        own_kernel,
        [pinned[0], pinned[2], pinned[4]] + on_chip(frame, near, up),
        [
            (VMEM, (2 * HALF, 2 * HALF), BF16),
            (VMEM, (2 * HALF, 2 * HALF), BF16),
            (VMEM, (2, HALF, HALF), F32),
            (VMEM, (2, 2, HALF, HALF), F32),
            (VMEM, (2, HALF, AGG), F32),
            square,
            (VMEM, (AGG, HALF), F32),
            tall,
            tall,
        ],
        [
            pltpu.SMEM((RB, K), jnp.int32),
            pltpu.VMEM((4, BS, K * BS), F32),
            pltpu.VMEM((BS, HALF), F32),
            pltpu.VMEM((4, 6, BS, 2 * BS), F32),
            pltpu.SemaphoreType.DMA((3,)),
        ],
    )
    side, far, moved, early, late = call(
        edge_kernel,
        on_chip(odd, inner, outer, cross, factors, near, own, below, above),
        [(VMEM, (HALF, AGG), F32), square, square] + [(VMEM, (3 * AGG, AGG), F32)] * 2,
    )
    odd_pairs = [(i, i + 1 if i % 2 else i - 1) for i in range(1, devices - 1)]
    even_pairs = [(i, i ^ 1) for i in range(devices)]
    early = lax.ppermute(early, axes, odd_pairs)
    late = lax.ppermute(late, axes, even_pairs)
    (part,) = call(
        middle_kernel,
        on_chip(a_high, a_low, factors, crossed, own, image, above, side, far, moved),
        [(VMEM, (AGG, 3 * AGG), F32)],
    )
    slots = call(
        finish_kernel,
        [(SMEM, neighbors), (SMEM, target)] + on_chip(odd, part, early, late),
        [(VMEM, (SLOT, 8, 2 * BS), F32)] * RB,
    )
    got = {0: slots[0]}
    for shift in SHIFTS:
        pairs = [(i, (i + shift) % RB) for i in range(RB)]
        got[shift] = lax.ppermute(slots[shift], "gy", pairs)
    rows_out = (HBM, (RB, SLOT - 1, 8, 2 * BS), F32)
    begun, found = call(
        unpack_first_kernel,
        on_chip(*[got[shift] for shift in EARLY]),
        [rows_out, (VMEM, (1, 2 * BS), F32)],
        [pltpu.SemaphoreType.DMA((len(EARLY),))],
    )
    tiles, ids = call(
        unpack_second_kernel,
        [(HBM, pltpu.with_memory_space_constraint(begun, pltpu.HBM))]
        + on_chip(found, *[got[shift] for shift in LATE]),
        [rows_out, (HBM, (RB,), jnp.int32)],
        [pltpu.VMEM((RB,), jnp.int32), pltpu.SemaphoreType.DMA((len(LATE) + 1,))],
        aliases={0: 0},
    )
    rows = tiles.reshape(RB * BS // 8, AW // 128, 8, 128).transpose(0, 2, 1, 3)
    return rows.reshape(RB * BS, AW), ids


def solution(mesh):
    placed = (
        P(("gx", "gy"), None, None),
        P(("gx", "gy"), None),
        P(("gx", "gy")),
        P(None, ("gx", "gy")),
        P(None, ("gx", "gy")),
        P(("gx", "gy")),
    )
    return jax.shard_map(
        body,
        mesh=mesh,
        in_specs=placed,
        out_specs=(P(("gx", "gy"), None), P(("gx", "gy"))),
        check_vma=False,
    )
```

```python
import jax
import jax.numpy as jnp
from jax import lax
from jax.experimental import pallas as pl
from jax.experimental.pallas import tpu as pltpu
from jax.sharding import PartitionSpec as P

BS = 64
K = 7
RB = 8
NA = 2
AW = 640
HALF = 256
AGG = NA * BS
UP = 9 * BS + 8 + HALF
DOWN = 2 * BS + 8
SLOT = 5 * BS // 8 + 1
OMEGA = 2.0 / 3.0
F32 = jnp.float32
BF16 = jnp.bfloat16


def split(x):
    high = x.astype(BF16)
    return high, (x - high.astype(F32)).astype(BF16)


def dot3(a, b, side=1):
    def dot(x, y):
        return lax.dot_general(x, y, (((side,), (0,)), ((), ())), preferred_element_type=F32)

    return dot(a[0], b[0]) + (dot(a[0], b[1]) + dot(a[1], b[0]))


def lane_half(rows):
    return lax.broadcasted_iota(jnp.int32, (rows, 2 * BS), 1) // BS


def doubled(pair):
    low = lane_half(BS) == 0
    other = pltpu.roll(pair, BS, 1)
    return jnp.where(low, pair, other), jnp.where(low, other, pair)


def place(pairs, members):
    half = lane_half(BS)
    rows = []
    for p, pair in enumerate(pairs):
        for q, block in enumerate(doubled(pair)):
            rows.append(jnp.where(half == members[2 * p + q], block, 0.0))
    return jnp.concatenate(rows, 0)


def block_diagonal(low, high):
    tall = jnp.concatenate([jnp.concatenate([low, high], 1)] * 4, 0)
    row = lax.broadcasted_iota(jnp.int32, tall.shape, 0) // BS
    column = lax.broadcasted_iota(jnp.int32, tall.shape, 1) // BS
    return jnp.where(row == column, tall, 0.0)


def piece(ref, c):
    return ref[c * BS : (c + 1) * BS]


def received_place(ref, members):
    rows = [ref[members + m : members + m + 1].astype(jnp.int32) for m in range(4)]
    return place([piece(ref, 0), piece(ref, 1)], rows)


def frame_columns(frame, columns):
    return jnp.concatenate([frame[:, c].reshape(HALF, 2 * BS) for c in columns], 1)


def doubled_row(blocks, i):
    copies = []
    for p in range(3):
        copies.extend(doubled(blocks[i, :, 2 * p * BS : 2 * (p + 1) * BS]))
    last = blocks[i, :, 6 * BS : 7 * BS]
    return copies + [jnp.concatenate([last, last], 1)]


def own_prolong(own_rows, near, inverse, rows):
    summed = dot3(own_rows, split(near))
    return near[rows] - OMEGA * dot3(inverse, split(summed))


def spread(nbr, blocks, frame, i, origin):
    half = lane_half(BS)
    row, mine = i % 4, i + 4 if i < 4 else i
    copies = doubled_row(blocks, row)
    for c in range(6):
        frame[row, c] = jnp.zeros((BS, 2 * BS), F32)
    frame[row, mine // 2] = jnp.where(half == mine % 2, copies[0], 0.0)
    for k in range(1, K):
        at = nbr[i, k] - origin
        column = at >> 1
        frame[row, column] = frame[row, column] + jnp.where(half == (at & 1), copies[k], 0.0)


def frame_kernel(
    nbr_in, agg_in, blocks_in, tent_in, dinv_in, frame, near, odd, up, down, nbr, agg, blocks, sems
):
    def pieces(source, first, out, at, sem):
        return [
            pltpu.make_async_copy(
                source.at[:, first + c * 128 : first + (c + 1) * 128],
                out.at[at + c * BS : at + (c + 1) * BS],
                sems.at[sem + c],
            )
            for c in range(2)
        ]

    small = [
        pltpu.make_async_copy(nbr_in, nbr, sems.at[0]),
        pltpu.make_async_copy(agg_in, agg, sems.at[1]),
    ]
    tents = pieces(tent_in, 0, down, 0, 2) + pieces(tent_in, HALF, up, 0, 4)
    dinvs = pieces(dinv_in, HALF, up, 2 * BS, 6)
    rows = [
        pltpu.make_async_copy(blocks_in.at[4 + i], blocks.at[i], sems.at[8 + i]) for i in range(4)
    ]
    for copy in small + tents + rows + dinvs:
        copy.start()
    for copy in small + tents:
        copy.wait()
    first = nbr[0, 0]
    members = [agg[j] - first // 4 for j in range(RB)]
    odd[...] = jnp.full((8, 2 * BS), (first // RB) & 1, jnp.int32)
    near[...] = place([piece(ref, c) for ref in (down, up) for c in range(2)], members)
    row = lax.broadcasted_iota(jnp.int32, (8, 2 * BS), 0)
    for out, at, mine in ((down, 2 * BS, members[:4]), (up, 9 * BS, members[4:])):
        value = jnp.zeros((8, 2 * BS), F32)
        for m, member in enumerate(mine):
            value = jnp.where(row == m, member.astype(F32), value)
        out[at : at + 8] = value
    for i in range(4):
        rows[i].wait()
        spread(nbr, blocks, frame, 4 + i, first)
    for copy in dinvs:
        copy.wait()
    low = lane_half(BS) == 0
    for c, value in enumerate(
        [frame[3, 4], frame[3, 5], frame[2, 4]]
        + [jnp.where(low, frame[2, 5], pltpu.roll(frame[0, 4], BS, 1)), frame[1, 4]]
    ):
        up[(4 + c) * BS : (5 + c) * BS] = value
    up[UP - HALF :] = own_prolong(
        split(frame_columns(frame, range(0, 4))),
        near[...],
        split(block_diagonal(piece(up, 2), piece(up, 3))),
        slice(HALF, 2 * HALF),
    )


def own_kernel(
    nbr_in,
    blocks_in,
    dinv_in,
    frame,
    near,
    up,
    a_high,
    a_low,
    factors,
    inner,
    outer,
    cross,
    crossed,
    own,
    image,
    nbr,
    blocks,
    dinv,
    low_frame,
    sems,
):
    copies = [
        pltpu.make_async_copy(nbr_in, nbr, sems.at[0]),
        pltpu.make_async_copy(blocks_in.at[:4], blocks, sems.at[1]),
        pltpu.make_async_copy(dinv_in.at[:, :HALF], dinv, sems.at[2]),
    ]
    for copy in copies:
        copy.start()
    upper = split(frame_columns(frame, range(0, 4)))
    inverse = [None, split(block_diagonal(piece(up, 2), piece(up, 3)))]
    edge = [None, split(frame_columns(frame, (4, 5)))]
    for copy in copies:
        copy.wait()
    for i in range(4):
        spread(nbr, blocks, low_frame, i, nbr[0, 0] - 4)
    lower = split(frame_columns(low_frame, range(2, 6)))
    inverse[0] = split(block_diagonal(dinv[:, :128], dinv[:, 128:]))
    edge[0] = split(frame_columns(low_frame, (0, 1)))
    a = [jnp.concatenate([x, y], 0) for x, y in zip(lower, upper)]
    a_high[...], a_low[...] = a
    c_low = own_prolong(lower, near[...], inverse[0], slice(0, HALF))
    both = []
    for s in range(2):
        factor = -OMEGA * dot3(inverse[s], edge[s])
        factors[s] = factor
        both.append(split(factor))
    prolong = jnp.concatenate([c_low, up[UP - HALF :]], 0)
    own[...] = prolong
    applied = dot3(a, split(prolong))
    image[...] = applied
    for t in range(2):
        columns = slice(t * HALF, (t + 1) * HALF)
        moved = dot3((a[0][:, columns], a[1][:, columns]), both[t])
        for s in range(2):
            inner[s, t] = dot3(both[s], split(moved[s * HALF : (s + 1) * HALF]), 0)
    for s in range(2):
        outer[s] = dot3(both[s], split(applied[s * HALF : (s + 1) * HALF]), 0)
    cross[...] = dot3(both[0], edge[0], 0)
    crossed[...] = dot3(split(c_low), edge[0], 0)


def above_kernel(a_high, a_low, factors, inner, outer, above, right, turned, late_terms):
    placed = split(received_place(above, 2 * BS))
    b_high = dot3(split(factors[1]), placed)
    right[: 2 * HALF] = dot3((a_high[:, HALF:], a_low[:, HALF:]), split(b_high))
    right[2 * HALF :] = dot3(split(inner[0, 1]), placed)
    turned[...] = dot3(split(inner[1, 0]), placed, 0)
    high = dot3(split(inner[1, 1]), placed)
    late_terms[...] = dot3(placed, split(jnp.concatenate([outer[1], high], 1)), 0)


def edge_kernel(
    odd,
    inner,
    outer,
    cross,
    factors,
    near,
    own,
    right,
    turned,
    late_terms,
    below,
    side,
    far,
    moved,
    early,
    late,
):
    placed = split(received_place(below, 9 * BS))
    low = lane_half(BS) == 0
    none = jnp.zeros((BS, 2 * BS), F32)
    seven = piece(below, 7)
    a_below = split(
        jnp.concatenate(
            [
                jnp.concatenate(row, 1)
                for row in [
                    [jnp.where(low, pltpu.roll(seven, BS, 1), 0.0), none],
                    [piece(below, 8), none],
                    [piece(below, 6), jnp.where(low, seven, 0.0)],
                    [piece(below, 4), piece(below, 5)],
                ]
            ],
            0,
        )
    )
    inverse = split(block_diagonal(piece(below, 2), piece(below, 3)))
    b_below = -OMEGA * dot3(inverse, split(dot3(a_below, split(near[:HALF]))))
    b_low = dot3(split(factors[0]), placed)
    image_low = dot3(a_below, split(jnp.concatenate([b_low, own[:HALF]], 1)))
    c_below = below[UP - HALF :]
    far_rows = jnp.concatenate([c_below, b_below], 1)
    side[...] = b_low
    far[...] = far_rows
    moved[...] = image_low
    across = dot3(split(cross[...]), split(far_rows))
    left = dot3(split(inner[0, 0]), placed) + across[:, :AGG]
    middle = outer[0] + across[:, AGG:]
    down_terms = dot3(
        placed, split(jnp.concatenate([left, middle, right[2 * HALF :]], 1)), 0
    )
    lower_terms = dot3(split(c_below), split(image_low), 0)
    up_first = dot3(split(turned[...]), placed, 0)
    upward = odd[:1] == 1
    for c in range(3):
        columns = slice(c * AGG, (c + 1) * AGG)
        down = down_terms[:, columns]
        if c < 2:
            down = down + lower_terms[:, columns]
        up = up_first if c == 0 else late_terms[:, (c - 1) * AGG : c * AGG]
        early[columns] = jnp.where(upward, up, down)
        late[columns] = jnp.where(upward, down, up)


def middle_kernel(
    a_high, a_low, crossed, own, image, right, side, far, moved, part
):
    left = dot3((a_high[:, :HALF], a_low[:, :HALF]), split(side[...]))
    middle = dot3(
        split(own[...]), split(jnp.concatenate([left, image[...], right[: 2 * HALF]], 1)), 0
    )
    lower = dot3(split(far[:, AGG:]), split(moved[...]), 0) + dot3(
        split(crossed[...]), split(far[...])
    )
    part[:, : 2 * AGG] = middle[:, : 2 * AGG] + lower
    part[:, 2 * AGG :] = middle[:, 2 * AGG :]


def finish_kernel(target, odd, part, early, late, *outs):
    here = lax.axis_index("gy")
    first_id = (lax.axis_index("gx") * RB + here) * NA
    upward = odd[:1] == 1
    below = [
        jnp.where(upward, late[c * AGG : (c + 1) * AGG], early[c * AGG : (c + 1) * AGG])
        for c in range(3)
    ]
    above = [
        jnp.where(upward, early[c * AGG : (c + 1) * AGG], late[c * AGG : (c + 1) * AGG])
        for c in range(3)
    ]
    band = [
        below[0],
        part[:, :AGG] + below[1],
        part[:, AGG : 2 * AGG] + below[2] + above[0],
        part[:, 2 * AGG :] + above[1],
        above[2],
    ]
    numbers = [jnp.full((8, 2 * BS), first_id + (u + 1), jnp.int32).astype(F32) for u in range(NA)]
    shifts = [(target[u] - here) & (RB - 1) for u in range(NA)]
    for shift, out in enumerate(outs):
        used = [jnp.full((8, 2 * BS), shifts[u], jnp.int32) == shift for u in range(NA)]

        def chosen(first, second):
            return jnp.where(used[0], first, jnp.where(used[1], second, 0.0))

        for r in range(8):
            for c in range(5):
                out[5 * r + c] = chosen(
                    *[band[c][u * BS + 8 * r : u * BS + 8 * (r + 1)] for u in range(NA)]
                )
        out[SLOT - 1] = chosen(*numbers)


def unpack(got, shifts, rows, sems, found):
    here = lax.axis_index("gy")
    copies = []
    sources = [(here - shift) & (RB - 1) for shift in shifts]
    for k, (source, ref) in enumerate(zip(sources, got)):
        copies.append(pltpu.make_async_copy(ref.at[: SLOT - 1], rows.at[source], sems.at[k]))
        copies[-1].start()
    lane = lax.broadcasted_iota(jnp.int32, (1, 2 * BS), 1)
    for source, ref in zip(sources, got):
        found = jnp.where(lane == source, ref[SLOT - 1, :1], found)
    return copies, found


def unpack_first_kernel(*refs):
    got, (rows, found, sems) = refs[: len(EARLY)], refs[len(EARLY) :]
    copies, numbers = unpack(got, EARLY, rows, sems, jnp.zeros((1, 2 * BS), F32))
    found[...] = numbers
    for copy in copies:
        copy.wait()


def unpack_second_kernel(begun, found, *refs):
    del begun
    got, (rows, ids, numbers, sems) = refs[: len(LATE)], refs[len(LATE) :]
    copies, held = unpack(got, LATE, rows, sems, found[...])
    numbers[...] = (held.astype(jnp.int32) - 1)[0, :RB]
    copies.append(pltpu.make_async_copy(numbers, ids, sems.at[len(LATE)]))
    copies[-1].start()
    for copy in copies:
        copy.wait()


SHIFTS = (4, 2, 6, 3, 5, 1, 7)
EARLY = (0,) + SHIFTS[:5]
LATE = SHIFTS[5:]


VMEM = pl.BlockSpec(memory_space=pltpu.VMEM)
SMEM = pl.BlockSpec(memory_space=pltpu.SMEM)
HBM = pl.BlockSpec(memory_space=pltpu.HBM)


def call(kernel, ins, outs, scratch=(), aliases=None):
    return pl.pallas_call(
        kernel,
        in_specs=[memory for memory, _ in ins],
        out_specs=[memory for memory, _, _ in outs],
        out_shape=[jax.ShapeDtypeStruct(shape, dtype) for _, shape, dtype in outs],
        scratch_shapes=list(scratch),
        input_output_aliases=aliases or {},
        compiler_params=pltpu.CompilerParams(vmem_limit_bytes=32 * 1024 * 1024),
        name=kernel.__name__,
    )(*[array for _, array in ins])


def on_chip(*arrays):
    return [(VMEM, array) for array in arrays]


def body(blocks, neighbors, aggregate, tentative, inv_diagonal, target):
    axes = ("gx", "gy")
    devices = lax.axis_size(axes)
    upward = [(i, i + 1) for i in range(devices - 1)]
    downward = [(j, i) for i, j in upward]
    tall = (VMEM, (2 * HALF, AGG), F32)
    square = (VMEM, (HALF, HALF), F32)
    pinned = [
        (HBM, pltpu.with_memory_space_constraint(x, pltpu.HBM))
        for x in (neighbors, aggregate, blocks, tentative, inv_diagonal)
    ]
    frame, near, odd, up, down = call(
        frame_kernel,
        pinned,
        [
            (VMEM, (4, 6, BS, 2 * BS), F32),
            tall,
            (VMEM, (8, 2 * BS), jnp.int32),
            (VMEM, (UP, 2 * BS), F32),
            (VMEM, (DOWN, 2 * BS), F32),
        ],
        [
            pltpu.SMEM((RB, K), jnp.int32),
            pltpu.SMEM((RB,), jnp.int32),
            pltpu.VMEM((4, BS, K * BS), F32),
            pltpu.SemaphoreType.DMA((12,)),
        ],
    )
    below = lax.ppermute(up, axes, upward)
    above = lax.ppermute(down, axes, downward)
    a_high, a_low, factors, inner, outer, cross, crossed, own, image = call(
        own_kernel,
        [pinned[0], pinned[2], pinned[4]] + on_chip(frame, near, up),
        [
            (VMEM, (2 * HALF, 2 * HALF), BF16),
            (VMEM, (2 * HALF, 2 * HALF), BF16),
            (VMEM, (2, HALF, HALF), F32),
            (VMEM, (2, 2, HALF, HALF), F32),
            (VMEM, (2, HALF, AGG), F32),
            square,
            (VMEM, (AGG, HALF), F32),
            tall,
            tall,
        ],
        [
            pltpu.SMEM((RB, K), jnp.int32),
            pltpu.VMEM((4, BS, K * BS), F32),
            pltpu.VMEM((BS, HALF), F32),
            pltpu.VMEM((4, 6, BS, 2 * BS), F32),
            pltpu.SemaphoreType.DMA((3,)),
        ],
    )
    right, turned, late_terms = call(
        above_kernel,
        on_chip(a_high, a_low, factors, inner, outer, above),
        [(VMEM, (3 * HALF, AGG), F32), (VMEM, (HALF, AGG), F32), (VMEM, (AGG, 2 * AGG), F32)],
    )
    side, far, moved, early, late = call(
        edge_kernel,
        on_chip(odd, inner, outer, cross, factors, near, own, right, turned, late_terms, below),
        [(VMEM, (HALF, AGG), F32), square, square] + [(VMEM, (3 * AGG, AGG), F32)] * 2,
    )
    odd_pairs = [(i, i + 1 if i % 2 else i - 1) for i in range(1, devices - 1)]
    even_pairs = [(i, i ^ 1) for i in range(devices)]
    early = lax.ppermute(early, axes, odd_pairs)
    late = lax.ppermute(late, axes, even_pairs)
    (part,) = call(
        middle_kernel,
        on_chip(a_high, a_low, crossed, own, image, right, side, far, moved),
        [(VMEM, (AGG, 3 * AGG), F32)],
    )
    slots = call(
        finish_kernel,
        [(SMEM, target)] + on_chip(odd, part, early, late),
        [(VMEM, (SLOT, 8, 2 * BS), F32)] * RB,
    )
    got = {0: slots[0]}
    for shift in SHIFTS:
        pairs = [(i, (i + shift) % RB) for i in range(RB)]
        got[shift] = lax.ppermute(slots[shift], "gy", pairs)
    rows_out = (HBM, (RB, SLOT - 1, 8, 2 * BS), F32)
    begun, found = call(
        unpack_first_kernel,
        on_chip(*[got[shift] for shift in EARLY]),
        [rows_out, (VMEM, (1, 2 * BS), F32)],
        [pltpu.SemaphoreType.DMA((len(EARLY),))],
    )
    tiles, ids = call(
        unpack_second_kernel,
        [(HBM, pltpu.with_memory_space_constraint(begun, pltpu.HBM))]
        + on_chip(found, *[got[shift] for shift in LATE]),
        [rows_out, (HBM, (RB,), jnp.int32)],
        [pltpu.VMEM((RB,), jnp.int32), pltpu.SemaphoreType.DMA((len(LATE) + 1,))],
        aliases={0: 0},
    )
    rows = tiles.reshape(RB * BS // 8, AW // 128, 8, 128).transpose(0, 2, 1, 3)
    return rows.reshape(RB * BS, AW), ids


def solution(mesh):
    placed = (
        P(("gx", "gy"), None, None),
        P(("gx", "gy"), None),
        P(("gx", "gy")),
        P(None, ("gx", "gy")),
        P(None, ("gx", "gy")),
        P(("gx", "gy")),
    )
    return jax.shard_map(
        body,
        mesh=mesh,
        in_specs=placed,
        out_specs=(P(("gx", "gy"), None), P(("gx", "gy"))),
        check_vma=False,
    )
```

```python
import jax
import jax.numpy as jnp
from jax import lax
from jax.experimental import pallas as pl
from jax.experimental.pallas import tpu as pltpu
from jax.sharding import PartitionSpec as P

BS = 64
K = 7
RB = 8
NA = 2
AW = 640
HALF = 256
AGG = NA * BS
UP = 9 * BS + 8 + HALF
DOWN = 2 * BS + 8
SLOT = 5 * BS // 8 + 1
OMEGA = 2.0 / 3.0
F32 = jnp.float32
BF16 = jnp.bfloat16


def split(x):
    high = x.astype(BF16)
    return high, (x - high.astype(F32)).astype(BF16)


def dot3(a, b, side=1):
    def dot(x, y):
        return lax.dot_general(x, y, (((side,), (0,)), ((), ())), preferred_element_type=F32)

    rows, columns = a[0].shape[1 - side], b[0].shape[1]
    if columns == AGG:
        both = dot(jnp.concatenate(a, 1 - side), jnp.concatenate(b, 1))
        return both[:rows, :columns] + (both[:rows, columns:] + both[rows:, :columns])
    both = dot(jnp.concatenate(a, 1 - side), b[0])
    return both[:rows] + (dot(a[0], b[1]) + both[rows:])


def lane_half(rows):
    return lax.broadcasted_iota(jnp.int32, (rows, 2 * BS), 1) // BS


def doubled(pair):
    low = lane_half(BS) == 0
    other = pltpu.roll(pair, BS, 1)
    return jnp.where(low, pair, other), jnp.where(low, other, pair)


def place(pairs, members):
    half = lane_half(BS)
    rows = []
    for p, pair in enumerate(pairs):
        for q, block in enumerate(doubled(pair)):
            rows.append(jnp.where(half == members[2 * p + q], block, 0.0))
    return jnp.concatenate(rows, 0)


def block_diagonal(low, high):
    tall = jnp.concatenate([jnp.concatenate([low, high], 1)] * 4, 0)
    row = lax.broadcasted_iota(jnp.int32, tall.shape, 0) // BS
    column = lax.broadcasted_iota(jnp.int32, tall.shape, 1) // BS
    return jnp.where(row == column, tall, 0.0)


def piece(ref, c):
    return ref[c * BS : (c + 1) * BS]


def received_place(ref, members):
    rows = [ref[members + m : members + m + 1].astype(jnp.int32) for m in range(4)]
    return place([piece(ref, 0), piece(ref, 1)], rows)


def frame_columns(frame, columns):
    return jnp.concatenate([frame[:, c].reshape(HALF, 2 * BS) for c in columns], 1)


def doubled_row(blocks, i):
    copies = []
    for p in range(3):
        copies.extend(doubled(blocks[i, :, 2 * p * BS : 2 * (p + 1) * BS]))
    last = blocks[i, :, 6 * BS : 7 * BS]
    return copies + [jnp.concatenate([last, last], 1)]


def own_prolong(own_rows, near, inverse, rows):
    summed = dot3(own_rows, split(near))
    return near[rows] - OMEGA * dot3(inverse, split(summed))


def spread(nbr, blocks, frame, i, origin):
    half = lane_half(BS)
    row, mine = i % 4, i + 4 if i < 4 else i
    copies = doubled_row(blocks, row)
    for c in range(6):
        frame[row, c] = jnp.zeros((BS, 2 * BS), F32)
    frame[row, mine // 2] = jnp.where(half == mine % 2, copies[0], 0.0)
    for k in range(1, K):
        at = nbr[i, k] - origin
        column = at >> 1
        frame[row, column] = frame[row, column] + jnp.where(half == (at & 1), copies[k], 0.0)


def frame_kernel(
    nbr_in, agg_in, blocks_in, tent_in, dinv_in, frame, near, odd, up, down, nbr, agg, blocks, sems
):
    def pieces(source, first, out, at, sem):
        return [
            pltpu.make_async_copy(
                source.at[:, first + c * 128 : first + (c + 1) * 128],
                out.at[at + c * BS : at + (c + 1) * BS],
                sems.at[sem + c],
            )
            for c in range(2)
        ]

    small = [
        pltpu.make_async_copy(nbr_in, nbr, sems.at[0]),
        pltpu.make_async_copy(agg_in, agg, sems.at[1]),
    ]
    tents = pieces(tent_in, 0, down, 0, 2) + pieces(tent_in, HALF, up, 0, 4)
    dinvs = pieces(dinv_in, HALF, up, 2 * BS, 6)
    rows = [
        pltpu.make_async_copy(blocks_in.at[4 + i], blocks.at[i], sems.at[8 + i]) for i in range(4)
    ]
    for copy in small + tents + rows + dinvs:
        copy.start()
    for copy in small + tents:
        copy.wait()
    first = nbr[0, 0]
    members = [agg[j] - first // 4 for j in range(RB)]
    odd[...] = jnp.full((8, 2 * BS), (first // RB) & 1, jnp.int32)
    near[...] = place([piece(ref, c) for ref in (down, up) for c in range(2)], members)
    row = lax.broadcasted_iota(jnp.int32, (8, 2 * BS), 0)
    for out, at, mine in ((down, 2 * BS, members[:4]), (up, 9 * BS, members[4:])):
        value = jnp.zeros((8, 2 * BS), F32)
        for m, member in enumerate(mine):
            value = jnp.where(row == m, member.astype(F32), value)
        out[at : at + 8] = value
    for i in range(4):
        rows[i].wait()
        spread(nbr, blocks, frame, 4 + i, first)
    for copy in dinvs:
        copy.wait()
    low = lane_half(BS) == 0
    for c, value in enumerate(
        [frame[3, 4], frame[3, 5], frame[2, 4]]
        + [jnp.where(low, frame[2, 5], pltpu.roll(frame[0, 4], BS, 1)), frame[1, 4]]
    ):
        up[(4 + c) * BS : (5 + c) * BS] = value
    up[UP - HALF :] = own_prolong(
        split(frame_columns(frame, range(0, 4))),
        near[...],
        split(block_diagonal(piece(up, 2), piece(up, 3))),
        slice(HALF, 2 * HALF),
    )


def own_kernel(
    nbr_in,
    blocks_in,
    dinv_in,
    frame,
    near,
    up,
    a_high,
    a_low,
    factors,
    inner,
    outer,
    cross,
    crossed,
    own,
    image,
    nbr,
    blocks,
    dinv,
    low_frame,
    sems,
):
    copies = [
        pltpu.make_async_copy(nbr_in, nbr, sems.at[0]),
        pltpu.make_async_copy(blocks_in.at[:4], blocks, sems.at[1]),
        pltpu.make_async_copy(dinv_in.at[:, :HALF], dinv, sems.at[2]),
    ]
    for copy in copies:
        copy.start()
    upper = split(frame_columns(frame, range(0, 4)))
    inverse = [None, split(block_diagonal(piece(up, 2), piece(up, 3)))]
    edge = [None, split(frame_columns(frame, (4, 5)))]
    for copy in copies:
        copy.wait()
    for i in range(4):
        spread(nbr, blocks, low_frame, i, nbr[0, 0] - 4)
    lower = split(frame_columns(low_frame, range(2, 6)))
    inverse[0] = split(block_diagonal(dinv[:, :128], dinv[:, 128:]))
    edge[0] = split(frame_columns(low_frame, (0, 1)))
    a = [jnp.concatenate([x, y], 0) for x, y in zip(lower, upper)]
    a_high[...], a_low[...] = a
    c_low = own_prolong(lower, near[...], inverse[0], slice(0, HALF))
    both = []
    for s in range(2):
        factor = -OMEGA * dot3(inverse[s], edge[s])
        factors[s] = factor
        both.append(split(factor))
    prolong = jnp.concatenate([c_low, up[UP - HALF :]], 0)
    own[...] = prolong
    applied = dot3(a, split(prolong))
    image[...] = applied
    for t in range(2):
        columns = slice(t * HALF, (t + 1) * HALF)
        moved = dot3((a[0][:, columns], a[1][:, columns]), both[t])
        for s in range(2):
            inner[s, t] = dot3(both[s], split(moved[s * HALF : (s + 1) * HALF]), 0)
    for s in range(2):
        outer[s] = dot3(both[s], split(applied[s * HALF : (s + 1) * HALF]), 0)
    cross[...] = dot3(both[0], edge[0], 0)
    crossed[...] = dot3(split(c_low), edge[0], 0)


def above_kernel(a_high, a_low, factors, inner, outer, above, right, turned, late_terms):
    placed = split(received_place(above, 2 * BS))
    b_high = dot3(split(factors[1]), placed)
    right[: 2 * HALF] = dot3((a_high[:, HALF:], a_low[:, HALF:]), split(b_high))
    right[2 * HALF :] = dot3(split(inner[0, 1]), placed)
    turned[...] = dot3(split(inner[1, 0]), placed, 0)
    high = dot3(split(inner[1, 1]), placed)
    late_terms[...] = dot3(placed, split(jnp.concatenate([outer[1], high], 1)), 0)


def edge_kernel(
    odd,
    inner,
    outer,
    cross,
    factors,
    near,
    own,
    right,
    turned,
    late_terms,
    below,
    side,
    far,
    moved,
    early,
    late,
):
    placed = split(received_place(below, 9 * BS))
    low = lane_half(BS) == 0
    none = jnp.zeros((BS, 2 * BS), F32)
    seven = piece(below, 7)
    a_below = split(
        jnp.concatenate(
            [
                jnp.concatenate(row, 1)
                for row in [
                    [jnp.where(low, pltpu.roll(seven, BS, 1), 0.0), none],
                    [piece(below, 8), none],
                    [piece(below, 6), jnp.where(low, seven, 0.0)],
                    [piece(below, 4), piece(below, 5)],
                ]
            ],
            0,
        )
    )
    inverse = split(block_diagonal(piece(below, 2), piece(below, 3)))
    b_below = -OMEGA * dot3(inverse, split(dot3(a_below, split(near[:HALF]))))
    b_low = dot3(split(factors[0]), placed)
    image_low = dot3(a_below, split(jnp.concatenate([b_low, own[:HALF]], 1)))
    c_below = below[UP - HALF :]
    far_rows = jnp.concatenate([c_below, b_below], 1)
    side[...] = b_low
    far[...] = far_rows
    moved[...] = image_low
    across = dot3(split(cross[...]), split(far_rows))
    left = dot3(split(inner[0, 0]), placed) + across[:, :AGG]
    middle = outer[0] + across[:, AGG:]
    down_terms = dot3(
        placed, split(jnp.concatenate([left, middle, right[2 * HALF :]], 1)), 0
    )
    lower_terms = dot3(split(c_below), split(image_low), 0)
    up_first = dot3(split(turned[...]), placed, 0)
    upward = odd[:1] == 1
    for c in range(3):
        columns = slice(c * AGG, (c + 1) * AGG)
        down = down_terms[:, columns]
        if c < 2:
            down = down + lower_terms[:, columns]
        up = up_first if c == 0 else late_terms[:, (c - 1) * AGG : c * AGG]
        early[columns] = jnp.where(upward, up, down)
        late[columns] = jnp.where(upward, down, up)


def middle_kernel(
    a_high, a_low, crossed, own, image, right, side, far, moved, part
):
    left = dot3((a_high[:, :HALF], a_low[:, :HALF]), split(side[...]))
    middle = dot3(
        split(own[...]), split(jnp.concatenate([left, image[...], right[: 2 * HALF]], 1)), 0
    )
    lower = dot3(split(far[:, AGG:]), split(moved[...]), 0) + dot3(
        split(crossed[...]), split(far[...])
    )
    part[:, : 2 * AGG] = middle[:, : 2 * AGG] + lower
    part[:, 2 * AGG :] = middle[:, 2 * AGG :]


def finish_kernel(target, odd, part, early, late, *outs):
    here = lax.axis_index("gy")
    first_id = (lax.axis_index("gx") * RB + here) * NA
    upward = odd[:1] == 1
    below = [
        jnp.where(upward, late[c * AGG : (c + 1) * AGG], early[c * AGG : (c + 1) * AGG])
        for c in range(3)
    ]
    above = [
        jnp.where(upward, early[c * AGG : (c + 1) * AGG], late[c * AGG : (c + 1) * AGG])
        for c in range(3)
    ]
    band = [
        below[0],
        part[:, :AGG] + below[1],
        part[:, AGG : 2 * AGG] + below[2] + above[0],
        part[:, 2 * AGG :] + above[1],
        above[2],
    ]
    numbers = [jnp.full((8, 2 * BS), first_id + (u + 1), jnp.int32).astype(F32) for u in range(NA)]
    shifts = [(target[u] - here) & (RB - 1) for u in range(NA)]
    for shift, out in enumerate(outs):
        used = [jnp.full((8, 2 * BS), shifts[u], jnp.int32) == shift for u in range(NA)]

        def chosen(first, second):
            return jnp.where(used[0], first, jnp.where(used[1], second, 0.0))

        for r in range(8):
            for c in range(5):
                out[5 * r + c] = chosen(
                    *[band[c][u * BS + 8 * r : u * BS + 8 * (r + 1)] for u in range(NA)]
                )
        out[SLOT - 1] = chosen(*numbers)


def unpack(got, shifts, rows, sems, found):
    here = lax.axis_index("gy")
    copies = []
    sources = [(here - shift) & (RB - 1) for shift in shifts]
    for k, (source, ref) in enumerate(zip(sources, got)):
        copies.append(pltpu.make_async_copy(ref.at[: SLOT - 1], rows.at[source], sems.at[k]))
        copies[-1].start()
    lane = lax.broadcasted_iota(jnp.int32, (1, 2 * BS), 1)
    for source, ref in zip(sources, got):
        found = jnp.where(lane == source, ref[SLOT - 1, :1], found)
    return copies, found


def unpack_first_kernel(*refs):
    got, (rows, found, sems) = refs[: len(EARLY)], refs[len(EARLY) :]
    copies, numbers = unpack(got, EARLY, rows, sems, jnp.zeros((1, 2 * BS), F32))
    found[...] = numbers
    for copy in copies:
        copy.wait()


def unpack_second_kernel(begun, found, *refs):
    del begun
    got, (rows, ids, numbers, sems) = refs[: len(LATE)], refs[len(LATE) :]
    copies, held = unpack(got, LATE, rows, sems, found[...])
    numbers[...] = (held.astype(jnp.int32) - 1)[0, :RB]
    copies.append(pltpu.make_async_copy(numbers, ids, sems.at[len(LATE)]))
    copies[-1].start()
    for copy in copies:
        copy.wait()


SHIFTS = (4, 2, 6, 3, 5, 1, 7)
EARLY = (0,) + SHIFTS[:5]
LATE = SHIFTS[5:]


VMEM = pl.BlockSpec(memory_space=pltpu.VMEM)
SMEM = pl.BlockSpec(memory_space=pltpu.SMEM)
HBM = pl.BlockSpec(memory_space=pltpu.HBM)


def call(kernel, ins, outs, scratch=(), aliases=None):
    return pl.pallas_call(
        kernel,
        in_specs=[memory for memory, _ in ins],
        out_specs=[memory for memory, _, _ in outs],
        out_shape=[jax.ShapeDtypeStruct(shape, dtype) for _, shape, dtype in outs],
        scratch_shapes=list(scratch),
        input_output_aliases=aliases or {},
        compiler_params=pltpu.CompilerParams(vmem_limit_bytes=32 * 1024 * 1024),
        name=kernel.__name__,
    )(*[array for _, array in ins])


def on_chip(*arrays):
    return [(VMEM, array) for array in arrays]


def body(blocks, neighbors, aggregate, tentative, inv_diagonal, target):
    axes = ("gx", "gy")
    devices = lax.axis_size(axes)
    upward = [(i, i + 1) for i in range(devices - 1)]
    downward = [(j, i) for i, j in upward]
    tall = (VMEM, (2 * HALF, AGG), F32)
    square = (VMEM, (HALF, HALF), F32)
    pinned = [
        (HBM, pltpu.with_memory_space_constraint(x, pltpu.HBM))
        for x in (neighbors, aggregate, blocks, tentative, inv_diagonal)
    ]
    frame, near, odd, up, down = call(
        frame_kernel,
        pinned,
        [
            (VMEM, (4, 6, BS, 2 * BS), F32),
            tall,
            (VMEM, (8, 2 * BS), jnp.int32),
            (VMEM, (UP, 2 * BS), F32),
            (VMEM, (DOWN, 2 * BS), F32),
        ],
        [
            pltpu.SMEM((RB, K), jnp.int32),
            pltpu.SMEM((RB,), jnp.int32),
            pltpu.VMEM((4, BS, K * BS), F32),
            pltpu.SemaphoreType.DMA((12,)),
        ],
    )
    below = lax.ppermute(up, axes, upward)
    above = lax.ppermute(down, axes, downward)
    a_high, a_low, factors, inner, outer, cross, crossed, own, image = call(
        own_kernel,
        [pinned[0], pinned[2], pinned[4]] + on_chip(frame, near, up),
        [
            (VMEM, (2 * HALF, 2 * HALF), BF16),
            (VMEM, (2 * HALF, 2 * HALF), BF16),
            (VMEM, (2, HALF, HALF), F32),
            (VMEM, (2, 2, HALF, HALF), F32),
            (VMEM, (2, HALF, AGG), F32),
            square,
            (VMEM, (AGG, HALF), F32),
            tall,
            tall,
        ],
        [
            pltpu.SMEM((RB, K), jnp.int32),
            pltpu.VMEM((4, BS, K * BS), F32),
            pltpu.VMEM((BS, HALF), F32),
            pltpu.VMEM((4, 6, BS, 2 * BS), F32),
            pltpu.SemaphoreType.DMA((3,)),
        ],
    )
    right, turned, late_terms = call(
        above_kernel,
        on_chip(a_high, a_low, factors, inner, outer, above),
        [(VMEM, (3 * HALF, AGG), F32), (VMEM, (HALF, AGG), F32), (VMEM, (AGG, 2 * AGG), F32)],
    )
    side, far, moved, early, late = call(
        edge_kernel,
        on_chip(odd, inner, outer, cross, factors, near, own, right, turned, late_terms, below),
        [(VMEM, (HALF, AGG), F32), square, square] + [(VMEM, (3 * AGG, AGG), F32)] * 2,
    )
    odd_pairs = [(i, i + 1 if i % 2 else i - 1) for i in range(1, devices - 1)]
    even_pairs = [(i, i ^ 1) for i in range(devices)]
    early = lax.ppermute(early, axes, odd_pairs)
    late = lax.ppermute(late, axes, even_pairs)
    (part,) = call(
        middle_kernel,
        on_chip(a_high, a_low, crossed, own, image, right, side, far, moved),
        [(VMEM, (AGG, 3 * AGG), F32)],
    )
    slots = call(
        finish_kernel,
        [(SMEM, target)] + on_chip(odd, part, early, late),
        [(VMEM, (SLOT, 8, 2 * BS), F32)] * RB,
    )
    got = {0: slots[0]}
    for shift in SHIFTS:
        pairs = [(i, (i + shift) % RB) for i in range(RB)]
        got[shift] = lax.ppermute(slots[shift], "gy", pairs)
    rows_out = (HBM, (RB, SLOT - 1, 8, 2 * BS), F32)
    begun, found = call(
        unpack_first_kernel,
        on_chip(*[got[shift] for shift in EARLY]),
        [rows_out, (VMEM, (1, 2 * BS), F32)],
        [pltpu.SemaphoreType.DMA((len(EARLY),))],
    )
    tiles, ids = call(
        unpack_second_kernel,
        [(HBM, pltpu.with_memory_space_constraint(begun, pltpu.HBM))]
        + on_chip(found, *[got[shift] for shift in LATE]),
        [rows_out, (HBM, (RB,), jnp.int32)],
        [pltpu.VMEM((RB,), jnp.int32), pltpu.SemaphoreType.DMA((len(LATE) + 1,))],
        aliases={0: 0},
    )
    rows = tiles.reshape(RB * BS // 8, AW // 128, 8, 128).transpose(0, 2, 1, 3)
    return rows.reshape(RB * BS, AW), ids


def solution(mesh):
    placed = (
        P(("gx", "gy"), None, None),
        P(("gx", "gy"), None),
        P(("gx", "gy")),
        P(None, ("gx", "gy")),
        P(None, ("gx", "gy")),
        P(("gx", "gy")),
    )
    return jax.shard_map(
        body,
        mesh=mesh,
        in_specs=placed,
        out_specs=(P(("gx", "gy"), None), P(("gx", "gy"))),
        check_vma=False,
    )
```

```python
import jax
import jax.numpy as jnp
from jax import lax
from jax.experimental import pallas as pl
from jax.experimental.pallas import tpu as pltpu
from jax.sharding import PartitionSpec as P

BS = 64
K = 7
RB = 8
NA = 2
AW = 640
HALF = 256
AGG = NA * BS
UP = 9 * BS + 8 + HALF
DOWN = 2 * BS + 8
SLOT = 5 * BS // 8 + 1
OMEGA = 2.0 / 3.0
F32 = jnp.float32
BF16 = jnp.bfloat16


def split(x):
    high = x.astype(BF16)
    return high, (x - high.astype(F32)).astype(BF16)


def dot3(a, b, side=1):
    def dot(x, y):
        return lax.dot_general(x, y, (((side,), (0,)), ((), ())), preferred_element_type=F32)

    rows, columns = a[0].shape[1 - side], b[0].shape[1]
    if columns == AGG:
        both = dot(jnp.concatenate(a, 1 - side), jnp.concatenate(b, 1))
        return both[:rows, :columns] + (both[:rows, columns:] + both[rows:, :columns])
    both = dot(jnp.concatenate(a, 1 - side), b[0])
    return both[:rows] + (dot(a[0], b[1]) + both[rows:])


def lane_half(rows):
    return lax.broadcasted_iota(jnp.int32, (rows, 2 * BS), 1) // BS


def doubled(pair):
    low = lane_half(BS) == 0
    other = pltpu.roll(pair, BS, 1)
    return jnp.where(low, pair, other), jnp.where(low, other, pair)


def place(pairs, members):
    half = lane_half(BS)
    rows = []
    for p, pair in enumerate(pairs):
        for q, block in enumerate(doubled(pair)):
            rows.append(jnp.where(half == members[2 * p + q], block, 0.0))
    return jnp.concatenate(rows, 0)


def block_diagonal(low, high):
    tall = jnp.concatenate([jnp.concatenate([low, high], 1)] * 4, 0)
    row = lax.broadcasted_iota(jnp.int32, tall.shape, 0) // BS
    column = lax.broadcasted_iota(jnp.int32, tall.shape, 1) // BS
    return jnp.where(row == column, tall, 0.0)


def piece(ref, c):
    return ref[c * BS : (c + 1) * BS]


def received_place(ref, members):
    rows = [ref[members + m : members + m + 1].astype(jnp.int32) for m in range(4)]
    return place([piece(ref, 0), piece(ref, 1)], rows)


def frame_columns(frame, columns):
    return jnp.concatenate([frame[:, c].reshape(HALF, 2 * BS) for c in columns], 1)


def doubled_row(blocks, i):
    copies = []
    for p in range(3):
        copies.extend(doubled(blocks[i, :, 2 * p * BS : 2 * (p + 1) * BS]))
    last = blocks[i, :, 6 * BS : 7 * BS]
    return copies + [jnp.concatenate([last, last], 1)]


def own_prolong(own_rows, near, inverse, rows):
    summed = dot3(own_rows, split(near))
    return near[rows] - OMEGA * dot3(inverse, split(summed))


def spread(nbr, blocks, frame, i, origin):
    half = lane_half(BS)
    row, mine = i % 4, i + 4 if i < 4 else i
    copies = doubled_row(blocks, row)
    for c in range(6):
        frame[row, c] = jnp.zeros((BS, 2 * BS), F32)
    frame[row, mine // 2] = jnp.where(half == mine % 2, copies[0], 0.0)
    for k in range(1, K):
        at = nbr[i, k] - origin
        column = at >> 1
        frame[row, column] = frame[row, column] + jnp.where(half == (at & 1), copies[k], 0.0)


def frame_kernel(
    nbr_in, agg_in, blocks_in, tent_in, dinv_in, frame, near, odd, up, down, nbr, agg, blocks, sems
):
    def pieces(source, first, out, at, sem):
        return [
            pltpu.make_async_copy(
                source.at[:, first + c * 128 : first + (c + 1) * 128],
                out.at[at + c * BS : at + (c + 1) * BS],
                sems.at[sem + c],
            )
            for c in range(2)
        ]

    small = [
        pltpu.make_async_copy(nbr_in, nbr, sems.at[0]),
        pltpu.make_async_copy(agg_in, agg, sems.at[1]),
    ]
    tents = pieces(tent_in, 0, down, 0, 2) + pieces(tent_in, HALF, up, 0, 4)
    dinvs = pieces(dinv_in, HALF, up, 2 * BS, 6)
    rows = [
        pltpu.make_async_copy(blocks_in.at[4 + i], blocks.at[i], sems.at[8 + i]) for i in range(4)
    ]
    for copy in small + tents + rows + dinvs:
        copy.start()
    for copy in small + tents:
        copy.wait()
    first = nbr[0, 0]
    members = [agg[j] - first // 4 for j in range(RB)]
    odd[...] = jnp.full((8, 2 * BS), (first // RB) & 1, jnp.int32)
    near[...] = place([piece(ref, c) for ref in (down, up) for c in range(2)], members)
    row = lax.broadcasted_iota(jnp.int32, (8, 2 * BS), 0)
    for out, at, mine in ((down, 2 * BS, members[:4]), (up, 9 * BS, members[4:])):
        value = jnp.zeros((8, 2 * BS), F32)
        for m, member in enumerate(mine):
            value = jnp.where(row == m, member.astype(F32), value)
        out[at : at + 8] = value
    for i in range(4):
        rows[i].wait()
        spread(nbr, blocks, frame, 4 + i, first)
    for copy in dinvs:
        copy.wait()
    low = lane_half(BS) == 0
    for c, value in enumerate(
        [frame[3, 4], frame[3, 5], frame[2, 4]]
        + [jnp.where(low, frame[2, 5], pltpu.roll(frame[0, 4], BS, 1)), frame[1, 4]]
    ):
        up[(4 + c) * BS : (5 + c) * BS] = value
    up[UP - HALF :] = own_prolong(
        split(frame_columns(frame, range(0, 4))),
        near[...],
        split(block_diagonal(piece(up, 2), piece(up, 3))),
        slice(HALF, 2 * HALF),
    )


def own_kernel(
    nbr_in,
    blocks_in,
    dinv_in,
    frame,
    near,
    up,
    a_high,
    a_low,
    factors,
    inner,
    outer,
    cross,
    crossed,
    own,
    image,
    nbr,
    blocks,
    dinv,
    low_frame,
    sems,
):
    copies = [
        pltpu.make_async_copy(nbr_in, nbr, sems.at[0]),
        pltpu.make_async_copy(blocks_in.at[:4], blocks, sems.at[1]),
        pltpu.make_async_copy(dinv_in.at[:, :HALF], dinv, sems.at[2]),
    ]
    for copy in copies:
        copy.start()
    upper = split(frame_columns(frame, range(0, 4)))
    inverse = [None, split(block_diagonal(piece(up, 2), piece(up, 3)))]
    edge = [None, split(frame_columns(frame, (4, 5)))]
    for copy in copies:
        copy.wait()
    for i in range(4):
        spread(nbr, blocks, low_frame, i, nbr[0, 0] - 4)
    lower = split(frame_columns(low_frame, range(2, 6)))
    inverse[0] = split(block_diagonal(dinv[:, :128], dinv[:, 128:]))
    edge[0] = split(frame_columns(low_frame, (0, 1)))
    a = [jnp.concatenate([x, y], 0) for x, y in zip(lower, upper)]
    a_high[...], a_low[...] = a
    c_low = own_prolong(lower, near[...], inverse[0], slice(0, HALF))
    both = []
    for s in range(2):
        factor = -OMEGA * dot3(inverse[s], edge[s])
        factors[s] = factor
        both.append(split(factor))
    prolong = jnp.concatenate([c_low, up[UP - HALF :]], 0)
    own[...] = prolong
    applied = dot3(a, split(prolong))
    image[...] = applied
    for t in range(2):
        columns = slice(t * HALF, (t + 1) * HALF)
        moved = dot3((a[0][:, columns], a[1][:, columns]), both[t])
        for s in range(2):
            inner[s, t] = dot3(both[s], split(moved[s * HALF : (s + 1) * HALF]), 0)
    for s in range(2):
        outer[s] = dot3(both[s], split(applied[s * HALF : (s + 1) * HALF]), 0)
    cross[...] = dot3(both[0], edge[0], 0)
    crossed[...] = dot3(split(c_low), edge[0], 0)


def above_kernel(a_high, a_low, factors, inner, outer, above, right, turned, late_terms):
    placed = split(received_place(above, 2 * BS))
    b_high = dot3(split(factors[1]), placed)
    right[: 2 * HALF] = dot3((a_high[:, HALF:], a_low[:, HALF:]), split(b_high))
    right[2 * HALF :] = dot3(split(inner[0, 1]), placed)
    turned[...] = dot3(split(inner[1, 0]), placed, 0)
    high = dot3(split(inner[1, 1]), placed)
    late_terms[...] = dot3(placed, split(jnp.concatenate([outer[1], high], 1)), 0)


def edge_kernel(
    odd,
    inner,
    outer,
    cross,
    factors,
    near,
    own,
    right,
    turned,
    late_terms,
    below,
    side,
    far,
    moved,
    early,
    late,
):
    placed = split(received_place(below, 9 * BS))
    low = lane_half(BS) == 0
    none = jnp.zeros((BS, 2 * BS), F32)
    seven = piece(below, 7)
    a_below = split(
        jnp.concatenate(
            [
                jnp.concatenate(row, 1)
                for row in [
                    [jnp.where(low, pltpu.roll(seven, BS, 1), 0.0), none],
                    [piece(below, 8), none],
                    [piece(below, 6), jnp.where(low, seven, 0.0)],
                    [piece(below, 4), piece(below, 5)],
                ]
            ],
            0,
        )
    )
    inverse = split(block_diagonal(piece(below, 2), piece(below, 3)))
    b_below = -OMEGA * dot3(inverse, split(dot3(a_below, split(near[:HALF]))))
    b_low = dot3(split(factors[0]), placed)
    image_low = dot3(a_below, split(jnp.concatenate([b_low, own[:HALF]], 1)))
    c_below = below[UP - HALF :]
    far_rows = jnp.concatenate([c_below, b_below], 1)
    side[...] = b_low
    far[...] = far_rows
    moved[...] = image_low
    across = dot3(split(cross[...]), split(far_rows))
    left = dot3(split(inner[0, 0]), placed) + across[:, :AGG]
    middle = outer[0] + across[:, AGG:]
    down_terms = dot3(
        placed, split(jnp.concatenate([left, middle, right[2 * HALF :]], 1)), 0
    )
    lower_terms = dot3(split(c_below), split(image_low), 0)
    up_first = dot3(split(turned[...]), placed, 0)
    upward = odd[:1] == 1
    for c in range(3):
        columns = slice(c * AGG, (c + 1) * AGG)
        down = down_terms[:, columns]
        if c < 2:
            down = down + lower_terms[:, columns]
        up = up_first if c == 0 else late_terms[:, (c - 1) * AGG : c * AGG]
        early[columns] = jnp.where(upward, up, down)
        late[columns] = jnp.where(upward, down, up)


def middle_kernel(
    a_high, a_low, crossed, own, image, right, side, far, moved, part
):
    left = dot3((a_high[:, :HALF], a_low[:, :HALF]), split(side[...]))
    middle = dot3(
        split(own[...]), split(jnp.concatenate([left, image[...], right[: 2 * HALF]], 1)), 0
    )
    lower = dot3(split(far[:, AGG:]), split(moved[...]), 0) + dot3(
        split(crossed[...]), split(far[...])
    )
    part[:, : 2 * AGG] = middle[:, : 2 * AGG] + lower
    part[:, 2 * AGG :] = middle[:, 2 * AGG :]


def fill(shifts_out, target, odd, part, early, late, outs):
    here = lax.axis_index("gy")
    first_id = (lax.axis_index("gx") * RB + here) * NA
    upward = odd[:1] == 1
    below = [
        jnp.where(upward, late[c * AGG : (c + 1) * AGG], early[c * AGG : (c + 1) * AGG])
        for c in range(3)
    ]
    above = [
        jnp.where(upward, early[c * AGG : (c + 1) * AGG], late[c * AGG : (c + 1) * AGG])
        for c in range(3)
    ]
    band = [
        below[0],
        part[:, :AGG] + below[1],
        part[:, AGG : 2 * AGG] + below[2] + above[0],
        part[:, 2 * AGG :] + above[1],
        above[2],
    ]
    numbers = [jnp.full((8, 2 * BS), first_id + (u + 1), jnp.int32).astype(F32) for u in range(NA)]
    shifts = [(target[u] - here) & (RB - 1) for u in range(NA)]
    for shift, out in zip(shifts_out, outs):
        used = [jnp.full((8, 2 * BS), shifts[u], jnp.int32) == shift for u in range(NA)]

        def chosen(first, second):
            return jnp.where(used[0], first, jnp.where(used[1], second, 0.0))

        for r in range(8):
            for c in range(5):
                out[5 * r + c] = chosen(
                    *[band[c][u * BS + 8 * r : u * BS + 8 * (r + 1)] for u in range(NA)]
                )
        out[SLOT - 1] = chosen(*numbers)


def finish_first_kernel(target, odd, part, early, late, *outs):
    fill(SHIFTS[:1], target, odd, part, early, late, outs)


def finish_rest_kernel(target, odd, part, early, late, *outs):
    fill((0,) + SHIFTS[1:], target, odd, part, early, late, outs)


def unpack(got, shifts, rows, sems, found):
    here = lax.axis_index("gy")
    copies = []
    sources = [(here - shift) & (RB - 1) for shift in shifts]
    for k, (source, ref) in enumerate(zip(sources, got)):
        copies.append(pltpu.make_async_copy(ref.at[: SLOT - 1], rows.at[source], sems.at[k]))
        copies[-1].start()
    lane = lax.broadcasted_iota(jnp.int32, (1, 2 * BS), 1)
    for source, ref in zip(sources, got):
        found = jnp.where(lane == source, ref[SLOT - 1, :1], found)
    return copies, found


def unpack_first_kernel(*refs):
    got, (rows, found, sems) = refs[: len(EARLY)], refs[len(EARLY) :]
    copies, numbers = unpack(got, EARLY, rows, sems, jnp.zeros((1, 2 * BS), F32))
    found[...] = numbers
    for copy in copies:
        copy.wait()


def unpack_second_kernel(begun, found, *refs):
    del begun
    got, (rows, ids, numbers, sems) = refs[: len(LATE)], refs[len(LATE) :]
    copies, held = unpack(got, LATE, rows, sems, found[...])
    numbers[...] = (held.astype(jnp.int32) - 1)[0, :RB]
    copies.append(pltpu.make_async_copy(numbers, ids, sems.at[len(LATE)]))
    copies[-1].start()
    for copy in copies:
        copy.wait()


SHIFTS = (4, 2, 6, 3, 5, 1, 7)
EARLY = (0,) + SHIFTS[:5]
LATE = SHIFTS[5:]


VMEM = pl.BlockSpec(memory_space=pltpu.VMEM)
SMEM = pl.BlockSpec(memory_space=pltpu.SMEM)
HBM = pl.BlockSpec(memory_space=pltpu.HBM)


def call(kernel, ins, outs, scratch=(), aliases=None):
    return pl.pallas_call(
        kernel,
        in_specs=[memory for memory, _ in ins],
        out_specs=[memory for memory, _, _ in outs],
        out_shape=[jax.ShapeDtypeStruct(shape, dtype) for _, shape, dtype in outs],
        scratch_shapes=list(scratch),
        input_output_aliases=aliases or {},
        compiler_params=pltpu.CompilerParams(vmem_limit_bytes=32 * 1024 * 1024),
        name=kernel.__name__,
    )(*[array for _, array in ins])


def on_chip(*arrays):
    return [(VMEM, array) for array in arrays]


def body(blocks, neighbors, aggregate, tentative, inv_diagonal, target):
    axes = ("gx", "gy")
    devices = lax.axis_size(axes)
    upward = [(i, i + 1) for i in range(devices - 1)]
    downward = [(j, i) for i, j in upward]
    tall = (VMEM, (2 * HALF, AGG), F32)
    square = (VMEM, (HALF, HALF), F32)
    pinned = [
        (HBM, pltpu.with_memory_space_constraint(x, pltpu.HBM))
        for x in (neighbors, aggregate, blocks, tentative, inv_diagonal)
    ]
    frame, near, odd, up, down = call(
        frame_kernel,
        pinned,
        [
            (VMEM, (4, 6, BS, 2 * BS), F32),
            tall,
            (VMEM, (8, 2 * BS), jnp.int32),
            (VMEM, (UP, 2 * BS), F32),
            (VMEM, (DOWN, 2 * BS), F32),
        ],
        [
            pltpu.SMEM((RB, K), jnp.int32),
            pltpu.SMEM((RB,), jnp.int32),
            pltpu.VMEM((4, BS, K * BS), F32),
            pltpu.SemaphoreType.DMA((12,)),
        ],
    )
    below = lax.ppermute(up, axes, upward)
    above = lax.ppermute(down, axes, downward)
    a_high, a_low, factors, inner, outer, cross, crossed, own, image = call(
        own_kernel,
        [pinned[0], pinned[2], pinned[4]] + on_chip(frame, near, up),
        [
            (VMEM, (2 * HALF, 2 * HALF), BF16),
            (VMEM, (2 * HALF, 2 * HALF), BF16),
            (VMEM, (2, HALF, HALF), F32),
            (VMEM, (2, 2, HALF, HALF), F32),
            (VMEM, (2, HALF, AGG), F32),
            square,
            (VMEM, (AGG, HALF), F32),
            tall,
            tall,
        ],
        [
            pltpu.SMEM((RB, K), jnp.int32),
            pltpu.VMEM((4, BS, K * BS), F32),
            pltpu.VMEM((BS, HALF), F32),
            pltpu.VMEM((4, 6, BS, 2 * BS), F32),
            pltpu.SemaphoreType.DMA((3,)),
        ],
    )
    right, turned, late_terms = call(
        above_kernel,
        on_chip(a_high, a_low, factors, inner, outer, above),
        [(VMEM, (3 * HALF, AGG), F32), (VMEM, (HALF, AGG), F32), (VMEM, (AGG, 2 * AGG), F32)],
    )
    side, far, moved, early, late = call(
        edge_kernel,
        on_chip(odd, inner, outer, cross, factors, near, own, right, turned, late_terms, below),
        [(VMEM, (HALF, AGG), F32), square, square] + [(VMEM, (3 * AGG, AGG), F32)] * 2,
    )
    odd_pairs = [(i, i + 1 if i % 2 else i - 1) for i in range(1, devices - 1)]
    even_pairs = [(i, i ^ 1) for i in range(devices)]
    early = lax.ppermute(early, axes, odd_pairs)
    late = lax.ppermute(late, axes, even_pairs)
    (part,) = call(
        middle_kernel,
        on_chip(a_high, a_low, crossed, own, image, right, side, far, moved),
        [(VMEM, (AGG, 3 * AGG), F32)],
    )
    got = {}
    for kernel, filled in (
        (finish_first_kernel, SHIFTS[:1]),
        (finish_rest_kernel, (0,) + SHIFTS[1:]),
    ):
        slots = call(
            kernel,
            [(SMEM, target)] + on_chip(odd, part, early, late),
            [(VMEM, (SLOT, 8, 2 * BS), F32)] * len(filled),
        )
        for shift, slot in zip(filled, slots):
            pairs = [(i, (i + shift) % RB) for i in range(RB)]
            got[shift] = lax.ppermute(slot, "gy", pairs) if shift else slot
    rows_out = (HBM, (RB, SLOT - 1, 8, 2 * BS), F32)
    begun, found = call(
        unpack_first_kernel,
        on_chip(*[got[shift] for shift in EARLY]),
        [rows_out, (VMEM, (1, 2 * BS), F32)],
        [pltpu.SemaphoreType.DMA((len(EARLY),))],
    )
    tiles, ids = call(
        unpack_second_kernel,
        [(HBM, pltpu.with_memory_space_constraint(begun, pltpu.HBM))]
        + on_chip(found, *[got[shift] for shift in LATE]),
        [rows_out, (HBM, (RB,), jnp.int32)],
        [pltpu.VMEM((RB,), jnp.int32), pltpu.SemaphoreType.DMA((len(LATE) + 1,))],
        aliases={0: 0},
    )
    rows = tiles.reshape(RB * BS // 8, AW // 128, 8, 128).transpose(0, 2, 1, 3)
    return rows.reshape(RB * BS, AW), ids


def solution(mesh):
    placed = (
        P(("gx", "gy"), None, None),
        P(("gx", "gy"), None),
        P(("gx", "gy")),
        P(None, ("gx", "gy")),
        P(None, ("gx", "gy")),
        P(("gx", "gy")),
    )
    return jax.shard_map(
        body,
        mesh=mesh,
        in_specs=placed,
        out_specs=(P(("gx", "gy"), None), P(("gx", "gy"))),
        check_vma=False,
    )
```
